32 devices in a mesh: seq: 8 (over z, y), head: 4 (over x, core).
Axes of the slice: x: 2, y: 2, z: 4, core: 2. Of those that a mesh axis runs over, the one named last changes fastest.
Arguments:
- queries: bfloat16 [2048, 4096], P('seq', 'head'), may hold values from -6 to 6
- keys: bfloat16 [2048, 512], P(('seq', 'head')), may hold values from -6 to 6
- values: bfloat16 [2048, 512], P(('seq', 'head')), may hold values from -6 to 6
- d_out: bfloat16 [2048, 4096], P('seq', 'head'), may hold values from -6 to 6
- rand_blocks: int32 [32, 8], P('seq'), may hold values from 0 to 31, as said below
- glob_blocks: int32 [2], replicated, may hold values from 0 to 31
Outputs:
- attn_out: bfloat16 [2048, 4096], P('seq', 'head')
- d_queries: bfloat16 [2048, 4096], P('seq', 'head')
- d_keys: bfloat16 [2048, 512], P(('seq', 'head'))
- d_values: bfloat16 [2048, 512], P(('seq', 'head'))
The draws below stay inside these ranges and needn't reach their ends.
Inputs may be any that keep to these rules, and one draw needn't show every extreme that they name: `rand_blocks`: block b lies on index b // 4 of seq. Among the 32 entries of the query blocks of one index of seq, at most 4 name blocks of any one index, and some index of seq reaches 4 for some owner in every draw.
All inputs are finite; a program needn't handle non-finite values.
Results may differ from the reference program's by a relative error of at most 0.012.
Values may be sent and summed in bfloat16 or wider, within the bound.
No kernel may reach another device: no remote copies, remote signals or barrier semaphores. Data moves between devices by JAX's collectives and lax.ppermute only.
A program may use at most 64 MiB of HBM per device.

```python
import jax
import jax.numpy as jnp
from jax import lax

DH = 128
QH = 32
KVH = 4
BLOCK = 64
GLOB = 2
RAND = 8
QB_DEV = 4
TOKENS = 2048
NB = 32
N_SEQ = 8


def drawn_pair(key):
    base = jax.random.fold_in(key, 7001)
    first_key, second_key = jax.random.split(base, 2)
    query_mat = jnp.clip(jax.random.normal(first_key, (TOKENS, QH * DH), jnp.float32), -6.0, 6.0)
    key_mat = jnp.clip(jax.random.normal(second_key, (TOKENS, KVH * DH), jnp.float32), -6.0, 6.0)
    return (query_mat, key_mat)


def draw_queries(key, part):
    query_mat, key_mat = drawn_pair(key)
    return query_mat.astype(jnp.bfloat16)


def draw_keys(key, part):
    query_mat, key_mat = drawn_pair(key)
    return key_mat.astype(jnp.bfloat16)


def draw_rand_blocks(key, part):
    base = jax.random.fold_in(key, 9001)
    popular_key, device_key, inner_key = jax.random.split(base, 3)
    capacity = (QB_DEV * RAND + N_SEQ - 1) // N_SEQ
    position_count = N_SEQ * capacity
    wanted = QB_DEV * RAND
    preferred_blocks = (jax.random.randint(popular_key, (N_SEQ,), 0, 8) == 0).astype(jnp.int32)
    position_holder = jnp.arange(position_count, dtype=jnp.int32) // capacity
    extra_score = preferred_blocks[position_holder] * 32768
    random_jitter = jax.random.randint(device_key, (N_SEQ, position_count), 0, 32768)
    sorted_order = (random_jitter + extra_score[None, :]) * position_count + jnp.arange(position_count, dtype=jnp.int32)[None, :]
    ignored, picked = lax.top_k(sorted_order, wanted)
    owners = picked // capacity
    inner = jax.random.randint(inner_key, (N_SEQ, wanted), 0, QB_DEV)
    chosen = owners * QB_DEV + inner
    return chosen.reshape(NB, RAND).astype(jnp.int32)


def steps_of(stream_key, extent, cuts, least, high):
    loudness = 1.0
    for dim, shards_of in cuts:
        steps = jax.random.uniform(jax.random.fold_in(jax.random.fold_in(stream_key, 6), dim), (shards_of,), jnp.float32, least / len(cuts), high / len(cuts))
        loudness = loudness * jnp.repeat(jnp.exp(steps), extent[dim] // shards_of).reshape((-1,) + (1,) * (len(extent) - 1 - dim))
    return loudness


def normal_values(stream_key, dims, scale, bound, cuts=(), held_as=jnp.bfloat16):
    values = scale * jax.random.normal(stream_key, dims, jnp.float32)
    if cuts:
        values = values * steps_of(stream_key, dims, cuts, -0.22, 0.18)
    return jnp.clip(values, -bound, bound).astype(held_as)


def setup_inputs(seed: int = 0) -> dict:
    streams_of = jax.random.split(jax.random.key(seed), 7)
    queries = draw_queries(jax.random.fold_in(streams_of[6], 71), 0)
    keys = draw_keys(jax.random.fold_in(streams_of[6], 71), 0)
    values = normal_values(streams_of[2], (TOKENS, KVH * DH), 1.0, 6.0, ((0, 32),))
    d_out = normal_values(streams_of[3], (TOKENS, QH * DH), 1.0, 6.0, ((0, 8), (1, 4)))
    rand_blocks = draw_rand_blocks(jax.random.fold_in(streams_of[6], 71), 0)
    glob_blocks = jax.random.randint(streams_of[5], (GLOB,), 0, NB).astype(jnp.int32)
    return {"queries": queries, "keys": keys, "values": values, "d_out": d_out, "rand_blocks": rand_blocks, "glob_blocks": glob_blocks}


def reference(queries, keys, values, d_out, rand_blocks, glob_blocks):
    factor = DH ** -0.5
    group = QH // KVH
    count = 3 + GLOB + RAND
    stacked = jnp.concatenate([keys.reshape(NB, BLOCK, KVH, DH), values.reshape(NB, BLOCK, KVH, DH)], axis=3)
    query_all = queries.reshape(NB, BLOCK, KVH, group, DH)
    grad_all = d_out.reshape(NB, BLOCK, KVH, group, DH)
    blocks = jnp.arange(NB, dtype=jnp.int32)
    window = jnp.stack([jnp.maximum(blocks - 1, 0), blocks, jnp.minimum(blocks + 1, NB - 1)], axis=1)
    lists = jnp.concatenate([window, jnp.broadcast_to(glob_blocks[None, :], (NB, GLOB)).astype(jnp.int32), rand_blocks.astype(jnp.int32)], axis=1).astype(jnp.int32)
    valid = jnp.concatenate([(blocks > 0)[:, None], jnp.ones((NB, 1), jnp.bool_), (blocks < NB - 1)[:, None], jnp.ones((NB, GLOB + RAND), jnp.bool_)], axis=1)
    crossing = (window // QB_DEV) != (blocks // QB_DEV)[:, None]
    rounded_flag = jnp.concatenate([crossing, jnp.zeros((NB, GLOB), jnp.bool_), jnp.ones((NB, RAND), jnp.bool_)], axis=1)

    def step(accum, inputs):
        query_block, gradient_tile, spots, allowed, rounding = inputs
        gathered = stacked[spots].astype(jnp.float32).reshape(count * BLOCK, KVH, 2 * DH)
        key_rows = gathered[:, :, :DH]
        value_rows = gathered[:, :, DH:]
        query32 = query_block.astype(jnp.float32)
        grad32 = gradient_tile.astype(jnp.float32)
        scores = jnp.einsum("tkgd,skd->kgts", query32, key_rows) * factor
        columns = jnp.repeat(allowed, BLOCK)
        scores = jnp.where(columns[None, None, None, :], scores, -1.0e30)
        peak = jnp.max(scores, axis=-1, keepdims=True)
        logsum = peak + jnp.log(jnp.sum(jnp.exp(scores - peak), axis=-1, keepdims=True))
        probs = jnp.exp(scores - logsum)
        probs16 = lax.optimization_barrier(probs.astype(jnp.bfloat16)).astype(jnp.float32)
        output = jnp.einsum("kgts,skd->tkgd", probs16, value_rows).astype(jnp.bfloat16)
        delta = jnp.sum(grad32 * output.astype(jnp.float32), axis=-1)
        dprobs = jnp.einsum("tkgd,skd->kgts", grad32, value_rows)
        dscores = probs * (dprobs - jnp.transpose(delta, (1, 2, 0))[..., None])
        dscores16 = lax.optimization_barrier(dscores.astype(jnp.bfloat16)).astype(jnp.float32)
        dquery = (jnp.einsum("kgts,skd->tkgd", dscores16, key_rows) * factor).astype(jnp.bfloat16)
        dkey = jnp.einsum("kgts,tkgd->skd", dscores16, query32) * factor
        dvalue = jnp.einsum("kgts,tkgd->skd", probs16, grad32)
        terms = jnp.concatenate([dkey, dvalue], axis=-1).reshape(count, BLOCK, KVH, 2 * DH)
        shipped = lax.optimization_barrier(terms.astype(jnp.bfloat16)).astype(jnp.float32)
        terms = jnp.where(rounding[:, None, None, None], shipped, terms)
        accum = accum.at[spots].add(terms)
        return accum, (output.reshape(BLOCK, QH * DH), dquery.reshape(BLOCK, QH * DH))

    start = jnp.zeros((NB, BLOCK, KVH, 2 * DH), jnp.float32)
    accum, (outputs, dqueries) = lax.scan(step, start, (query_all, grad_all, lists, valid, rounded_flag))
    d_keys = accum[..., :DH].astype(jnp.bfloat16).reshape(TOKENS, KVH * DH)
    d_values = accum[..., DH:].astype(jnp.bfloat16).reshape(TOKENS, KVH * DH)
    return outputs.reshape(TOKENS, QH * DH), dqueries.reshape(TOKENS, QH * DH), d_keys, d_values
```

```python
import math

import jax
import jax.numpy as jnp
from jax import lax
from jax.experimental import pallas as pl
from jax.experimental.pallas import tpu as pltpu
from jax.sharding import PartitionSpec as P

DH = 128
KVH = 4
BLOCK = 64
GLOB = 2
RAND = 8


NEG_FILL = -1e30


def padded_2(cells, sides, width):
    for axis, dim in sides:
        count = lax.axis_size(axis)
        ends = count - 1
        head = lax.slice_in_dim(cells, 0, width, axis=dim)
        tail = lax.slice_in_dim(cells, cells.shape[dim] - width, cells.shape[dim], axis=dim)
        cells = jnp.concatenate(
            [
                lax.ppermute(tail, axis, [(i, (i + 1) % count) for i in range(ends)]),
                cells,
                lax.ppermute(head, axis, [((i + 1) % count, i) for i in range(ends)]),
            ],
            axis=dim,
        )
    return cells


def broadcast(block, axis, source):
    block = jnp.where(lax.axis_index(axis) == source, block, jnp.zeros_like(block))
    return lax.psum(block, axis)


def key_rows(library, spots):
    chosen = jnp.stack(
        [
            lax.dynamic_index_in_dim(library, spots[i], 0, keepdims=False)
            for i in range(spots.shape[0])
        ]
    )
    flat = chosen.reshape(chosen.shape[0] * chosen.shape[1], chosen.shape[2])
    return (flat[:, :DH], flat[:, DH:])


def masked_scores(query_block, keys_here, allowed_row):
    factor = DH ** (-0.5)
    scores = (
        jnp.einsum("thd,kd->htk", query_block, keys_here, preferred_element_type=jnp.float32)
        * factor
    )
    widened = jnp.repeat(allowed_row, keys_here.shape[0] // allowed_row.shape[0])
    return jnp.where(widened[None, None, :], scores, NEG_FILL)


def request_body(queries, keys, values, d_out, rand_blocks, glob_blocks):
    seq_count = lax.axis_size("seq")
    here = lax.axis_index("seq")
    short = keys.shape[0]
    stacked = jnp.concatenate(
        [keys.reshape(short, KVH, DH), values.reshape(short, KVH, DH)], axis=2
    )
    mine = lax.all_to_all(stacked, "head", split_axis=1, concat_axis=0, tiled=True)
    tok_count = mine.shape[0]
    blocks_here = tok_count // BLOCK
    flat_pairs = mine.reshape(tok_count, 2 * DH)
    own_blocks = flat_pairs.reshape(blocks_here, BLOCK, 2 * DH)
    padded = padded_2(flat_pairs, (("seq", 0),), BLOCK)
    window = padded.reshape(blocks_here + 2, BLOCK, 2 * DH)
    global_parts = []
    for number in range(GLOB):
        target = glob_blocks[number]
        piece = lax.dynamic_index_in_dim(own_blocks, target % blocks_here, 0, keepdims=False)
        global_parts.append(broadcast(piece, "seq", target // blocks_here))
    global_pairs = jnp.stack(global_parts)
    entries = rand_blocks.reshape(-1)
    entry_count = entries.shape[0]
    capacity = -(-entry_count // seq_count)
    position_count = seq_count * capacity
    owners = entries // blocks_here
    inner_index = entries % blocks_here
    order = jnp.arange(entry_count, dtype=jnp.int32)
    earlier = (owners[:, None] == owners[None, :]) & (order[:, None] > order[None, :])
    ranks = jnp.sum(earlier.astype(jnp.int32), axis=1)
    slots = owners * capacity + ranks
    placing = slots[None, :] == jnp.arange(position_count, dtype=jnp.int32)[:, None]
    wanted = jnp.sum(jnp.where(placing, inner_index[None, :], 0), axis=1).reshape(
        seq_count, capacity
    )
    incoming = lax.all_to_all(wanted, "seq", split_axis=0, concat_axis=0, tiled=True).reshape(
        position_count
    )
    block_ids = jnp.arange(blocks_here, dtype=jnp.int32)
    picking = (incoming[:, None] == block_ids[None, :]).astype(jnp.bfloat16)
    served = (
        jnp.dot(
            picking,
            own_blocks.reshape(blocks_here, BLOCK * 2 * DH),
            preferred_element_type=jnp.float32,
        )
        .astype(jnp.bfloat16)
        .reshape(seq_count, capacity, BLOCK, 2 * DH)
    )
    fetched = lax.all_to_all(served, "seq", split_axis=0, concat_axis=0, tiled=True).reshape(
        position_count, BLOCK, 2 * DH
    )
    window_ids = jnp.stack([block_ids, block_ids + 1, block_ids + 2], axis=1)
    global_ids = jnp.broadcast_to(
        blocks_here + 2 + jnp.arange(GLOB, dtype=jnp.int32), (blocks_here, GLOB)
    )
    random_ids = blocks_here + 2 + GLOB + slots.reshape(blocks_here, RAND)
    positions = jnp.concatenate([window_ids, global_ids, random_ids], axis=1)
    allowed = jnp.concatenate(
        [
            jnp.logical_not((block_ids == 0) & (here == 0))[:, None],
            jnp.ones((blocks_here, 1), jnp.bool_),
            jnp.logical_not((block_ids == blocks_here - 1) & (here == seq_count - 1))[:, None],
            jnp.ones((blocks_here, GLOB + RAND), jnp.bool_),
        ],
        axis=1,
    )
    library = jnp.concatenate([window, global_pairs, fetched], axis=0)
    heads_here = queries.shape[1] // DH
    query_blocks = queries.reshape(blocks_here, BLOCK, heads_here, DH)
    grad_blocks = d_out.reshape(blocks_here, BLOCK, heads_here, DH)

    def forward_step(inputs):
        query_block, spots, allowed_row = inputs
        keys_here, values_here = key_rows(library, spots)
        scores = masked_scores(query_block, keys_here, allowed_row)
        peak = jnp.max(scores, axis=-1, keepdims=True)
        logsum = peak + jnp.log(jnp.sum(jnp.exp(scores - peak), axis=-1, keepdims=True))
        probs16 = jnp.exp(scores - logsum).astype(jnp.bfloat16)
        result = jnp.einsum("htk,kd->thd", probs16, values_here, preferred_element_type=jnp.float32)
        return (result.astype(jnp.bfloat16), logsum)

    out_blocks, logsums = lax.map(forward_step, (query_blocks, positions, allowed))
    refetched = lax.all_to_all(served, "seq", split_axis=0, concat_axis=0, tiled=True).reshape(
        position_count, BLOCK, 2 * DH
    )
    library_back = jnp.concatenate([window, global_pairs, refetched], axis=0)

    def backward_step(inputs):
        query_block, gradient_tile, out_block, logsum, spots, allowed_row = inputs
        keys_here, values_here = key_rows(library_back, spots)
        factor = DH ** (-0.5)
        scores = masked_scores(query_block, keys_here, allowed_row)
        probs = jnp.exp(scores - logsum)
        probs16 = probs.astype(jnp.bfloat16)
        delta = jnp.sum(gradient_tile.astype(jnp.float32) * out_block.astype(jnp.float32), axis=-1)
        dprobs = jnp.einsum(
            "thd,kd->htk", gradient_tile, values_here, preferred_element_type=jnp.float32
        )
        dscores = (probs * (dprobs - jnp.transpose(delta)[:, :, None])).astype(jnp.bfloat16)
        dquery = (
            jnp.einsum("htk,kd->thd", dscores, keys_here, preferred_element_type=jnp.float32)
            * factor
        )
        dkey = (
            jnp.einsum("htk,thd->kd", dscores, query_block, preferred_element_type=jnp.float32)
            * factor
        )
        dvalue = jnp.einsum(
            "htk,thd->kd", probs16, gradient_tile, preferred_element_type=jnp.float32
        )
        terms = jnp.concatenate([dkey, dvalue], axis=1).reshape(spots.shape[0], BLOCK, 2 * DH)
        return (dquery.astype(jnp.bfloat16), terms)

    dquery_blocks, terms = lax.map(
        backward_step, (query_blocks, grad_blocks, out_blocks, logsums, positions, allowed)
    )
    attn_out = out_blocks.reshape(tok_count, heads_here * DH)
    d_queries = dquery_blocks.reshape(tok_count, heads_here * DH)
    prev_terms = terms[:, 0]
    self_terms = terms[:, 1]
    next_terms = terms[:, 2]
    zero_block = jnp.zeros((1, BLOCK, 2 * DH), jnp.float32)
    grads = (
        self_terms
        + jnp.concatenate([prev_terms[1:], zero_block], axis=0)
        + jnp.concatenate([zero_block, next_terms[:-1]], axis=0)
    )
    rims = jnp.concatenate([prev_terms[0], next_terms[-1]], axis=0).astype(jnp.bfloat16)
    arrived = padded_2(rims, (("seq", 0),), BLOCK)
    from_left = arrived[:BLOCK].astype(jnp.float32)
    from_right = arrived[3 * BLOCK :].astype(jnp.float32)
    edge_first = jnp.concatenate(
        [from_left[None], jnp.zeros((blocks_here - 1, BLOCK, 2 * DH), jnp.float32)], axis=0
    )
    edge_last = jnp.concatenate(
        [jnp.zeros((blocks_here - 1, BLOCK, 2 * DH), jnp.float32), from_right[None]], axis=0
    )
    grads = grads + edge_first + edge_last
    global_terms = jnp.sum(terms[:, 3 : 3 + GLOB], axis=0)
    global_total = lax.psum(global_terms, "seq")
    global_hits = ((glob_blocks // blocks_here)[:, None] == here) & (
        (glob_blocks % blocks_here)[:, None] == block_ids[None, :]
    )
    grads = grads + jnp.sum(
        jnp.where(global_hits[:, :, None, None], global_total[:, None], 0.0), axis=0
    )
    random_terms = terms[:, 3 + GLOB :].reshape(entry_count, BLOCK * 2 * DH).astype(jnp.bfloat16)
    outgoing = jnp.dot(
        placing.astype(jnp.bfloat16), random_terms, preferred_element_type=jnp.float32
    ).astype(jnp.bfloat16)
    returned = lax.all_to_all(
        outgoing.reshape(seq_count, capacity, BLOCK, 2 * DH),
        "seq",
        split_axis=0,
        concat_axis=0,
        tiled=True,
    )
    landing = (incoming[None, :] == block_ids[:, None]).astype(jnp.bfloat16)
    grads = grads + jnp.dot(
        landing,
        returned.reshape(position_count, BLOCK * 2 * DH),
        preferred_element_type=jnp.float32,
    ).reshape(blocks_here, BLOCK, 2 * DH)
    packed = grads.astype(jnp.bfloat16).reshape(tok_count, 1, 2 * DH)
    restored = lax.all_to_all(packed, "head", split_axis=0, concat_axis=1, tiled=True)
    d_keys = restored[:, :, :DH].reshape(short, KVH * DH)
    d_values = restored[:, :, DH:].reshape(short, KVH * DH)
    return (attn_out, d_queries, d_keys, d_values)


def flips(count, bits):
    return [(i, i ^ bits) for i in range(count)]


def head_columns(head, offset):
    return pl.ds(pl.multiple_of((head ^ offset) * DH, DH), DH)


def pack_kernel(keys_ref, values_ref, *piece_refs):
    head = lax.axis_index("head")
    short = keys_ref.shape[0]
    for offset, piece in enumerate(piece_refs):
        columns = head_columns(head, offset)
        piece[:short, :] = keys_ref[:, columns]
        piece[short:, :] = values_ref[:, columns]


def unpack_kernel(*refs):
    piece_refs, (keys_ref, values_ref) = refs[:-2], refs[-2:]
    head = lax.axis_index("head")
    short = keys_ref.shape[0]
    for offset, piece in enumerate(piece_refs):
        columns = head_columns(head, offset)
        keys_ref[:, columns] = piece[:short, :]
        values_ref[:, columns] = piece[short:, :]


def dot(left, right, left_dim, right_dim):
    return lax.dot_general(
        left,
        right,
        (((left_dim,), (right_dim,)), ((), ())),
        preferred_element_type=jnp.float32,
    )


def attention_kernel(seq_count, chunk_heads, *refs):
    rand_ref, glob_ref, query_ref, grad_ref = refs[:4]
    part_refs = refs[4 : 4 + seq_count]
    out_ref, dquery_ref, keep_ref, ship_ref = refs[4 + seq_count : 8 + seq_count]
    library, total, key_rows_ref, value_rows_ref, sems = refs[8 + seq_count :]
    blocks_here = part_refs[0].shape[0]
    all_blocks = seq_count * blocks_here
    heads_here = query_ref.shape[1] // DH
    step = pl.program_id(0)
    here = lax.axis_index("seq")
    head = lax.axis_index("head")

    @pl.when(step == 0)
    def _():
        copies = [
            pltpu.make_async_copy(
                part, library.at[pl.ds(k * blocks_here, blocks_here)], sems.at[k]
            )
            for k, part in enumerate(part_refs)
        ]
        for copy in copies:
            copy.start()
        total[...] = jnp.zeros_like(total)
        for copy in copies:
            copy.wait()

    block = here * blocks_here + step
    names = [jnp.maximum(block - 1, 0), block, jnp.minimum(block + 1, all_blocks - 1)]
    names += [glob_ref[i] for i in range(GLOB)]
    names += [rand_ref[step, i] for i in range(RAND)]
    spots = []
    for name in names:
        owner = lax.div(name, blocks_here)
        inner = lax.rem(name, blocks_here)
        spots.append((owner ^ here) * blocks_here + (inner ^ head))
    for number, spot in enumerate(spots):
        rows = pl.ds(number * BLOCK, BLOCK)
        key_rows_ref[rows, :] = library[spot, :BLOCK, :]
        value_rows_ref[rows, :] = library[spot, BLOCK:, :]
    first_bias = jnp.where(block == 0, NEG_FILL, 0.0)
    last_bias = jnp.where(block == all_blocks - 1, NEG_FILL, 0.0)
    factor = DH ** (-0.5)
    scale = factor * math.log2(math.e)
    dkey = None
    for start in range(0, heads_here, chunk_heads):
        chunk = range(start, start + chunk_heads)
        query = jnp.concatenate([query_ref[:, h * DH : (h + 1) * DH] for h in chunk], axis=0)
        grad = jnp.concatenate([grad_ref[:, h * DH : (h + 1) * DH] for h in chunk], axis=0)
        scores = dot(key_rows_ref[...], query, 1, 1)
        scores = jnp.concatenate(
            [
                scores[:BLOCK] + first_bias,
                scores[BLOCK : 2 * BLOCK],
                scores[2 * BLOCK : 3 * BLOCK] + last_bias,
                scores[3 * BLOCK :],
            ],
            axis=0,
        )
        peak = jnp.max(scores, axis=0, keepdims=True)
        weights = jnp.exp2((scores - peak) * scale)
        probs = weights * (1.0 / jnp.sum(weights, axis=0, keepdims=True))
        probs16 = probs.astype(jnp.bfloat16)
        result = dot(value_rows_ref[...], probs16, 0, 0).astype(jnp.bfloat16)
        grad_across = jnp.transpose(grad.astype(jnp.float32))
        delta = jnp.sum(grad_across * result.astype(jnp.float32), axis=0, keepdims=True)
        dprobs = dot(value_rows_ref[...], grad, 1, 1)
        dscores = (probs * (dprobs - delta)).astype(jnp.bfloat16)
        dquery = dot(key_rows_ref[...], dscores, 0, 0) * factor
        result_down = jnp.transpose(result.astype(jnp.float32)).astype(jnp.bfloat16)
        dquery_down = jnp.transpose(dquery).astype(jnp.bfloat16)
        for number, h in enumerate(chunk):
            rows = slice(number * BLOCK, (number + 1) * BLOCK)
            out_ref[:, h * DH : (h + 1) * DH] = result_down[rows]
            dquery_ref[:, h * DH : (h + 1) * DH] = dquery_down[rows]
        key_term = dot(dscores, query, 1, 0) * factor
        value_term = dot(probs16, grad, 1, 0)
        dkey = key_term if dkey is None else dkey + key_term
        dvalue = value_term if start == 0 else dvalue + value_term
    for number, spot in enumerate(spots):
        rows = slice(number * BLOCK, (number + 1) * BLOCK)
        total[spot, :BLOCK, :] += dkey[rows]
        total[spot, BLOCK:, :] += dvalue[rows]

    @pl.when(step == pl.num_programs(0) - 1)
    def _():
        for pair in range(seq_count // 2):
            near = pl.ds(2 * pair * blocks_here, blocks_here)
            far = pl.ds((2 * pair + 1) * blocks_here, blocks_here)
            keep_ref[pair] = total[near]
            ship_ref[pair] = total[far].astype(jnp.bfloat16)


def attention(rand_blocks, glob_blocks, queries, d_out, parts):
    seq_count = len(parts)
    blocks_here, pair_rows, _ = parts[0].shape
    entries = 3 + GLOB + RAND
    tok_count, width = queries.shape
    heads_here = width // DH
    tile = pl.BlockSpec((BLOCK, width), lambda i: (i, 0))
    smem = pl.BlockSpec(memory_space=pltpu.SMEM)
    half = (seq_count // 2, blocks_here, pair_rows, DH)
    whole = pl.BlockSpec(half, lambda i: (0, 0, 0, 0))
    all_blocks = seq_count * blocks_here
    pairs = tok_count * heads_here * entries * BLOCK
    return pl.pallas_call(
        lambda *refs: attention_kernel(seq_count, math.gcd(heads_here, 4), *refs),
        grid=(blocks_here,),
        in_specs=[smem, smem, tile, tile] + [pl.BlockSpec(memory_space=pl.ANY)] * seq_count,
        out_specs=[tile, tile, whole, whole],
        out_shape=[
            jax.ShapeDtypeStruct(queries.shape, jnp.bfloat16),
            jax.ShapeDtypeStruct(queries.shape, jnp.bfloat16),
            jax.ShapeDtypeStruct(half, jnp.float32),
            jax.ShapeDtypeStruct(half, jnp.bfloat16),
        ],
        scratch_shapes=[
            pltpu.VMEM((all_blocks, pair_rows, DH), jnp.bfloat16),
            pltpu.VMEM((all_blocks, pair_rows, DH), jnp.float32),
            pltpu.VMEM((entries * BLOCK, DH), jnp.bfloat16),
            pltpu.VMEM((entries * BLOCK, DH), jnp.bfloat16),
            pltpu.SemaphoreType.DMA((seq_count,)),
        ],
        compiler_params=pltpu.CompilerParams(vmem_limit_bytes=40 * 1024 * 1024),
        cost_estimate=pl.CostEstimate(
            flops=12 * pairs * DH, bytes_accessed=8 * tok_count * width, transcendentals=pairs
        ),
    )(rand_blocks, glob_blocks, queries, d_out, *parts)


def whole_body(queries, keys, values, d_out, rand_blocks, glob_blocks):
    seq_count = lax.axis_size("seq")
    head_count = lax.axis_size("head")
    short = keys.shape[0]
    piece = jax.ShapeDtypeStruct((2 * short, DH), jnp.bfloat16)
    pieces = pl.pallas_call(pack_kernel, out_shape=[piece] * head_count)(keys, values)
    own = jnp.stack(
        [pieces[0]]
        + [
            lax.ppermute(pieces[k], "head", flips(head_count, k)) for k in range(1, head_count)
        ]
    )
    parts = {0: own}
    for k in range(seq_count - 2, 0, -2):
        parts[k] = lax.ppermute(own, "seq", flips(seq_count, k))
    for k in range(0, seq_count, 2):
        parts[k + 1] = lax.ppermute(parts[k], "seq", flips(seq_count, 1))
    attn_out, d_queries, keep, ship = attention(
        rand_blocks, glob_blocks, queries, d_out, [parts[k] for k in range(seq_count)]
    )
    pairs = seq_count // 2
    half = max(pairs // 2, 1)
    sums = {}
    for low in range(pairs - half, -1, -half):
        arrived = lax.ppermute(ship[low : low + half], "seq", flips(seq_count, 1))
        for number in range(half):
            pair = low + number
            sums[pair] = keep[pair] + arrived[number].astype(jnp.float32)
    total = sums[0]
    for pair in range(pairs - 1, 0, -1):
        total = total + lax.ppermute(
            sums[pair].astype(jnp.bfloat16), "seq", flips(seq_count, 2 * pair)
        ).astype(jnp.float32)
    packed = total.astype(jnp.bfloat16)
    back = [packed[0]] + [
        lax.ppermute(packed[k], "head", flips(head_count, k)) for k in range(1, head_count)
    ]
    flat = jax.ShapeDtypeStruct(keys.shape, jnp.bfloat16)
    d_keys, d_values = pl.pallas_call(unpack_kernel, out_shape=[flat, flat])(*back)
    return (attn_out, d_queries, d_keys, d_values)


def body(queries, keys, values, d_out, rand_blocks, glob_blocks):
    seq_count = lax.axis_size("seq")
    head_count = lax.axis_size("head")
    blocks_here = rand_blocks.shape[0]
    capacity = -(-rand_blocks.size // seq_count)
    powers = all(n & (n - 1) == 0 for n in (seq_count, head_count))
    fits = keys.shape[0] == BLOCK and blocks_here == head_count
    if capacity >= blocks_here and seq_count > 1 and powers and fits:
        return whole_body(queries, keys, values, d_out, rand_blocks, glob_blocks)
    return request_body(queries, keys, values, d_out, rand_blocks, glob_blocks)


def solution(mesh):
    in_specs = (
        P("seq", "head"),
        P(("seq", "head"), None),
        P(("seq", "head"), None),
        P("seq", "head"),
        P("seq", None),
        P(),
    )
    out_specs = (
        P("seq", "head"),
        P("seq", "head"),
        P(("seq", "head"), None),
        P(("seq", "head"), None),
    )
    return jax.shard_map(body, mesh=mesh, in_specs=in_specs, out_specs=out_specs, check_vma=False)
```

```python
import math

import jax
import jax.numpy as jnp
from jax import lax
from jax.experimental import pallas as pl
from jax.experimental.pallas import tpu as pltpu
from jax.sharding import PartitionSpec as P

DH = 128
KVH = 4
BLOCK = 64
GLOB = 2
RAND = 8


NEG_FILL = -1e30


def padded_2(cells, sides, width):
    for axis, dim in sides:
        count = lax.axis_size(axis)
        ends = count - 1
        head = lax.slice_in_dim(cells, 0, width, axis=dim)
        tail = lax.slice_in_dim(cells, cells.shape[dim] - width, cells.shape[dim], axis=dim)
        cells = jnp.concatenate(
            [
                lax.ppermute(tail, axis, [(i, (i + 1) % count) for i in range(ends)]),
                cells,
                lax.ppermute(head, axis, [((i + 1) % count, i) for i in range(ends)]),
            ],
            axis=dim,
        )
    return cells


def broadcast(block, axis, source):
    block = jnp.where(lax.axis_index(axis) == source, block, jnp.zeros_like(block))
    return lax.psum(block, axis)


def key_rows(library, spots):
    chosen = jnp.stack(
        [
            lax.dynamic_index_in_dim(library, spots[i], 0, keepdims=False)
            for i in range(spots.shape[0])
        ]
    )
    flat = chosen.reshape(chosen.shape[0] * chosen.shape[1], chosen.shape[2])
    return (flat[:, :DH], flat[:, DH:])


def masked_scores(query_block, keys_here, allowed_row):
    factor = DH ** (-0.5)
    scores = (
        jnp.einsum("thd,kd->htk", query_block, keys_here, preferred_element_type=jnp.float32)
        * factor
    )
    widened = jnp.repeat(allowed_row, keys_here.shape[0] // allowed_row.shape[0])
    return jnp.where(widened[None, None, :], scores, NEG_FILL)


def request_body(queries, keys, values, d_out, rand_blocks, glob_blocks):
    seq_count = lax.axis_size("seq")
    here = lax.axis_index("seq")
    short = keys.shape[0]
    stacked = jnp.concatenate(
        [keys.reshape(short, KVH, DH), values.reshape(short, KVH, DH)], axis=2
    )
    mine = lax.all_to_all(stacked, "head", split_axis=1, concat_axis=0, tiled=True)
    tok_count = mine.shape[0]
    blocks_here = tok_count // BLOCK
    flat_pairs = mine.reshape(tok_count, 2 * DH)
    own_blocks = flat_pairs.reshape(blocks_here, BLOCK, 2 * DH)
    padded = padded_2(flat_pairs, (("seq", 0),), BLOCK)
    window = padded.reshape(blocks_here + 2, BLOCK, 2 * DH)
    global_parts = []
    for number in range(GLOB):
        target = glob_blocks[number]
        piece = lax.dynamic_index_in_dim(own_blocks, target % blocks_here, 0, keepdims=False)
        global_parts.append(broadcast(piece, "seq", target // blocks_here))
    global_pairs = jnp.stack(global_parts)
    entries = rand_blocks.reshape(-1)
    entry_count = entries.shape[0]
    capacity = -(-entry_count // seq_count)
    position_count = seq_count * capacity
    owners = entries // blocks_here
    inner_index = entries % blocks_here
    order = jnp.arange(entry_count, dtype=jnp.int32)
    earlier = (owners[:, None] == owners[None, :]) & (order[:, None] > order[None, :])
    ranks = jnp.sum(earlier.astype(jnp.int32), axis=1)
    slots = owners * capacity + ranks
    placing = slots[None, :] == jnp.arange(position_count, dtype=jnp.int32)[:, None]
    wanted = jnp.sum(jnp.where(placing, inner_index[None, :], 0), axis=1).reshape(
        seq_count, capacity
    )
    incoming = lax.all_to_all(wanted, "seq", split_axis=0, concat_axis=0, tiled=True).reshape(
        position_count
    )
    block_ids = jnp.arange(blocks_here, dtype=jnp.int32)
    picking = (incoming[:, None] == block_ids[None, :]).astype(jnp.bfloat16)
    served = (
        jnp.dot(
            picking,
            own_blocks.reshape(blocks_here, BLOCK * 2 * DH),
            preferred_element_type=jnp.float32,
        )
        .astype(jnp.bfloat16)
        .reshape(seq_count, capacity, BLOCK, 2 * DH)
    )
    fetched = lax.all_to_all(served, "seq", split_axis=0, concat_axis=0, tiled=True).reshape(
        position_count, BLOCK, 2 * DH
    )
    window_ids = jnp.stack([block_ids, block_ids + 1, block_ids + 2], axis=1)
    global_ids = jnp.broadcast_to(
        blocks_here + 2 + jnp.arange(GLOB, dtype=jnp.int32), (blocks_here, GLOB)
    )
    random_ids = blocks_here + 2 + GLOB + slots.reshape(blocks_here, RAND)
    positions = jnp.concatenate([window_ids, global_ids, random_ids], axis=1)
    allowed = jnp.concatenate(
        [
            jnp.logical_not((block_ids == 0) & (here == 0))[:, None],
            jnp.ones((blocks_here, 1), jnp.bool_),
            jnp.logical_not((block_ids == blocks_here - 1) & (here == seq_count - 1))[:, None],
            jnp.ones((blocks_here, GLOB + RAND), jnp.bool_),
        ],
        axis=1,
    )
    library = jnp.concatenate([window, global_pairs, fetched], axis=0)
    heads_here = queries.shape[1] // DH
    query_blocks = queries.reshape(blocks_here, BLOCK, heads_here, DH)
    grad_blocks = d_out.reshape(blocks_here, BLOCK, heads_here, DH)

    def forward_step(inputs):
        query_block, spots, allowed_row = inputs
        keys_here, values_here = key_rows(library, spots)
        scores = masked_scores(query_block, keys_here, allowed_row)
        peak = jnp.max(scores, axis=-1, keepdims=True)
        logsum = peak + jnp.log(jnp.sum(jnp.exp(scores - peak), axis=-1, keepdims=True))
        probs16 = jnp.exp(scores - logsum).astype(jnp.bfloat16)
        result = jnp.einsum("htk,kd->thd", probs16, values_here, preferred_element_type=jnp.float32)
        return (result.astype(jnp.bfloat16), logsum)

    out_blocks, logsums = lax.map(forward_step, (query_blocks, positions, allowed))
    refetched = lax.all_to_all(served, "seq", split_axis=0, concat_axis=0, tiled=True).reshape(
        position_count, BLOCK, 2 * DH
    )
    library_back = jnp.concatenate([window, global_pairs, refetched], axis=0)

    def backward_step(inputs):
        query_block, gradient_tile, out_block, logsum, spots, allowed_row = inputs
        keys_here, values_here = key_rows(library_back, spots)
        factor = DH ** (-0.5)
        scores = masked_scores(query_block, keys_here, allowed_row)
        probs = jnp.exp(scores - logsum)
        probs16 = probs.astype(jnp.bfloat16)
        delta = jnp.sum(gradient_tile.astype(jnp.float32) * out_block.astype(jnp.float32), axis=-1)
        dprobs = jnp.einsum(
            "thd,kd->htk", gradient_tile, values_here, preferred_element_type=jnp.float32
        )
        dscores = (probs * (dprobs - jnp.transpose(delta)[:, :, None])).astype(jnp.bfloat16)
        dquery = (
            jnp.einsum("htk,kd->thd", dscores, keys_here, preferred_element_type=jnp.float32)
            * factor
        )
        dkey = (
            jnp.einsum("htk,thd->kd", dscores, query_block, preferred_element_type=jnp.float32)
            * factor
        )
        dvalue = jnp.einsum(
            "htk,thd->kd", probs16, gradient_tile, preferred_element_type=jnp.float32
        )
        terms = jnp.concatenate([dkey, dvalue], axis=1).reshape(spots.shape[0], BLOCK, 2 * DH)
        return (dquery.astype(jnp.bfloat16), terms)

    dquery_blocks, terms = lax.map(
        backward_step, (query_blocks, grad_blocks, out_blocks, logsums, positions, allowed)
    )
    attn_out = out_blocks.reshape(tok_count, heads_here * DH)
    d_queries = dquery_blocks.reshape(tok_count, heads_here * DH)
    prev_terms = terms[:, 0]
    self_terms = terms[:, 1]
    next_terms = terms[:, 2]
    zero_block = jnp.zeros((1, BLOCK, 2 * DH), jnp.float32)
    grads = (
        self_terms
        + jnp.concatenate([prev_terms[1:], zero_block], axis=0)
        + jnp.concatenate([zero_block, next_terms[:-1]], axis=0)
    )
    rims = jnp.concatenate([prev_terms[0], next_terms[-1]], axis=0).astype(jnp.bfloat16)
    arrived = padded_2(rims, (("seq", 0),), BLOCK)
    from_left = arrived[:BLOCK].astype(jnp.float32)
    from_right = arrived[3 * BLOCK :].astype(jnp.float32)
    edge_first = jnp.concatenate(
        [from_left[None], jnp.zeros((blocks_here - 1, BLOCK, 2 * DH), jnp.float32)], axis=0
    )
    edge_last = jnp.concatenate(
        [jnp.zeros((blocks_here - 1, BLOCK, 2 * DH), jnp.float32), from_right[None]], axis=0
    )
    grads = grads + edge_first + edge_last
    global_terms = jnp.sum(terms[:, 3 : 3 + GLOB], axis=0)
    global_total = lax.psum(global_terms, "seq")
    global_hits = ((glob_blocks // blocks_here)[:, None] == here) & (
        (glob_blocks % blocks_here)[:, None] == block_ids[None, :]
    )
    grads = grads + jnp.sum(
        jnp.where(global_hits[:, :, None, None], global_total[:, None], 0.0), axis=0
    )
    random_terms = terms[:, 3 + GLOB :].reshape(entry_count, BLOCK * 2 * DH).astype(jnp.bfloat16)
    outgoing = jnp.dot(
        placing.astype(jnp.bfloat16), random_terms, preferred_element_type=jnp.float32
    ).astype(jnp.bfloat16)
    returned = lax.all_to_all(
        outgoing.reshape(seq_count, capacity, BLOCK, 2 * DH),
        "seq",
        split_axis=0,
        concat_axis=0,
        tiled=True,
    )
    landing = (incoming[None, :] == block_ids[:, None]).astype(jnp.bfloat16)
    grads = grads + jnp.dot(
        landing,
        returned.reshape(position_count, BLOCK * 2 * DH),
        preferred_element_type=jnp.float32,
    ).reshape(blocks_here, BLOCK, 2 * DH)
    packed = grads.astype(jnp.bfloat16).reshape(tok_count, 1, 2 * DH)
    restored = lax.all_to_all(packed, "head", split_axis=0, concat_axis=1, tiled=True)
    d_keys = restored[:, :, :DH].reshape(short, KVH * DH)
    d_values = restored[:, :, DH:].reshape(short, KVH * DH)
    return (attn_out, d_queries, d_keys, d_values)


def flips(count, bits):
    return [(i, i ^ bits) for i in range(count)]


def head_columns(head, offset):
    return pl.ds(pl.multiple_of((head ^ offset) * DH, DH), DH)


def pack_kernel(seq_count, head_count, *refs):
    rand_from, glob_from, keys_ref, values_ref, query_ref, grad_ref = refs[:6]
    piece_refs = refs[6 : 6 + head_count]
    spots_ref, query_out, grad_out, rand_ref, glob_ref, sems = refs[6 + head_count :]
    here = lax.axis_index("seq")
    head = lax.axis_index("head")
    short = keys_ref.shape[0]
    copies = [(rand_from, rand_ref), (glob_from, glob_ref)]
    for offset, piece in enumerate(piece_refs):
        columns = head_columns(head, offset)
        copies.append((keys_ref.at[:, columns], piece.at[pl.ds(0, short)]))
        copies.append((values_ref.at[:, columns], piece.at[pl.ds(short, short)]))
    copies += [(query_ref, query_out), (grad_ref, grad_out)]
    copies = [pltpu.make_async_copy(a, b, sems.at[n]) for n, (a, b) in enumerate(copies)]
    for copy in copies:
        copy.start()
    copies[0].wait()
    copies[1].wait()
    blocks_here = rand_ref.shape[0]
    last = seq_count * blocks_here - 1
    for step in range(blocks_here):
        block = here * blocks_here + step
        names = [jnp.maximum(block - 1, 0), block, jnp.minimum(block + 1, last)]
        names += [glob_ref[i] for i in range(GLOB)]
        names += [rand_ref[step, i] for i in range(RAND)]
        for number, name in enumerate(names):
            owner = lax.div(name, blocks_here) ^ here
            slot = lax.rem(owner, 2) * (seq_count // 2) + lax.div(owner, 2)
            spots_ref[step, number] = slot * blocks_here + (lax.rem(name, blocks_here) ^ head)
    for copy in copies[2:]:
        copy.wait()


def unpack_kernel(*refs):
    piece_refs, (keys_ref, values_ref) = refs[:-2], refs[-2:]
    head = lax.axis_index("head")
    short = keys_ref.shape[0]
    for offset, piece in enumerate(piece_refs):
        columns = head_columns(head, offset)
        keys_ref[:, columns] = piece[:short, :]
        values_ref[:, columns] = piece[short:, :]


def dot(left, right, left_dim, right_dim):
    return lax.dot_general(
        left,
        right,
        (((left_dim,), (right_dim,)), ((), ())),
        preferred_element_type=jnp.float32,
    )


def load_parts(part_refs, library, sems):
    copies, at = [], 0
    for part in part_refs:
        size = part.shape[0]
        copies.append(
            pltpu.make_async_copy(part, library.at[pl.ds(at, size)], sems.at[len(copies)])
        )
        at += size
    return copies


def listed_spots(spots_ref, step):
    return [spots_ref[step, number] for number in range(spots_ref.shape[1])]


def begin(step, part_refs, library, total, sems):
    @pl.when(step == 0)
    def _():
        copies = load_parts(part_refs, library, sems)
        for copy in copies:
            copy.start()
        total[...] = jnp.zeros_like(total)
        for copy in copies:
            copy.wait()


def add_terms(total, spots, terms):
    for number, spot in enumerate(spots):
        total[spot] += terms[number * BLOCK : (number + 1) * BLOCK]


def finish(step, total, keep_ref, ship_ref):
    pairs, size = keep_ref.shape[:2]

    @pl.when(step == pl.num_programs(0) - 1)
    def _():
        for pair in range(pairs):
            keep_ref[pair] = total[pl.ds(pair * size, size)]
            ship_ref[pair] = total[pl.ds((pairs + pair) * size, size)].astype(jnp.bfloat16)


def stacked_heads(ref, chunk):
    return jnp.concatenate([ref[:, h * DH : (h + 1) * DH] for h in chunk], axis=0)


def chunks_of(heads, size):
    return [range(start, start + size) for start in range(0, heads, size)]


def probs_kernel(seq_count, size, *refs):
    spots_ref, query_ref, grad_ref = refs[:3]
    part_refs = refs[3 : 3 + seq_count]
    probs_ref, rows_ref, keep_ref, ship_ref, library, total, sems = refs[3 + seq_count :]
    blocks_here = part_refs[0].shape[0]
    all_blocks = seq_count * blocks_here
    step = pl.program_id(0)
    begin(step, part_refs, library, total, sems)
    block = lax.axis_index("seq") * blocks_here + step
    spots = listed_spots(spots_ref, step)
    for number, spot in enumerate(spots):
        rows_ref[0, pl.ds(number * BLOCK, BLOCK), :] = library[spot]
    first_bias = jnp.where(block == 0, NEG_FILL, 0.0)
    last_bias = jnp.where(block == all_blocks - 1, NEG_FILL, 0.0)
    scale = DH ** (-0.5) * math.log2(math.e)
    terms = 0.0
    for chunk in chunks_of(query_ref.shape[1] // DH, size):
        query = stacked_heads(query_ref, chunk)
        grad = stacked_heads(grad_ref, chunk)
        scores = dot(rows_ref[0], query, 1, 1)
        scores = jnp.concatenate(
            [
                scores[:BLOCK] + first_bias,
                scores[BLOCK : 2 * BLOCK],
                scores[2 * BLOCK : 3 * BLOCK] + last_bias,
                scores[3 * BLOCK :],
            ],
            axis=0,
        )
        peak = jnp.max(scores, axis=0, keepdims=True)
        weights = jnp.exp2((scores - peak) * scale)
        probs = weights * (1.0 / jnp.sum(weights, axis=0, keepdims=True))
        probs16 = probs.astype(jnp.bfloat16)
        probs_ref[0, :, chunk[0] * BLOCK : (chunk[-1] + 1) * BLOCK] = probs16
        terms = terms + dot(probs16, grad, 1, 0)
    add_terms(total, spots, terms)
    finish(step, total, keep_ref, ship_ref)


def dscores_kernel(size, *refs):
    spots_ref, query_ref, grad_ref, probs_ref = refs[:4]
    part_refs, refs = refs[4:-8], refs[-8:]
    out_ref, dscores_ref, keep_ref, ship_ref, library, total, rows_ref, sems = refs
    step = pl.program_id(0)
    begin(step, part_refs, library, total, sems)
    spots = listed_spots(spots_ref, step)
    for number, spot in enumerate(spots):
        rows_ref[pl.ds(number * BLOCK, BLOCK), :] = library[spot]
    terms = 0.0
    for chunk in chunks_of(query_ref.shape[1] // DH, size):
        columns = slice(chunk[0] * BLOCK, (chunk[-1] + 1) * BLOCK)
        query = stacked_heads(query_ref, chunk)
        grad = stacked_heads(grad_ref, chunk)
        probs16 = probs_ref[0, :, columns]
        result = dot(rows_ref[...], probs16, 0, 0).astype(jnp.bfloat16).astype(jnp.float32)
        grad_across = jnp.transpose(grad.astype(jnp.float32))
        delta = jnp.sum(grad_across * result, axis=0, keepdims=True)
        dprobs = dot(rows_ref[...], grad, 1, 1)
        dscores = (probs16.astype(jnp.float32) * (dprobs - delta)).astype(jnp.bfloat16)
        dscores_ref[0, :, columns] = dscores
        terms = terms + dot(dscores, query, 1, 0)
        down = jnp.transpose(result).astype(jnp.bfloat16)
        for number, h in enumerate(chunk):
            out_ref[:, h * DH : (h + 1) * DH] = down[number * BLOCK : (number + 1) * BLOCK]
    add_terms(total, spots, terms * DH ** (-0.5))
    finish(step, total, keep_ref, ship_ref)


def dquery_kernel(size, dscores_ref, rows_ref, dquery_ref):
    for chunk in chunks_of(dquery_ref.shape[1] // DH, size):
        columns = slice(chunk[0] * BLOCK, (chunk[-1] + 1) * BLOCK)
        across = dot(rows_ref[0], dscores_ref[0, :, columns], 0, 0) * DH ** (-0.5)
        down = jnp.transpose(across).astype(jnp.bfloat16)
        for number, h in enumerate(chunk):
            dquery_ref[:, h * DH : (h + 1) * DH] = down[number * BLOCK : (number + 1) * BLOCK]


def small_grant():
    return pltpu.CompilerParams(vmem_limit_bytes=8 * 1024 * 1024)


def kernel_options(products, pairs):
    return {
        "compiler_params": pltpu.CompilerParams(vmem_limit_bytes=40 * 1024 * 1024),
        "cost_estimate": pl.CostEstimate(
            flops=4 * products * pairs * DH, bytes_accessed=4 * pairs, transcendentals=pairs
        ),
    }


def whole_body(queries, keys, values, d_out, rand_blocks, glob_blocks):
    seq_count = lax.axis_size("seq")
    head_count = lax.axis_size("head")
    short = keys.shape[0]
    tok_count, width = queries.shape
    heads_here = width // DH
    blocks_here = tok_count // BLOCK
    pair_count = seq_count // 2
    listed = (3 + GLOB + RAND) * BLOCK
    columns = heads_here * BLOCK
    pairs = blocks_here * listed * columns
    size = math.gcd(heads_here, 4)

    smem = pl.BlockSpec(memory_space=pltpu.SMEM)
    anywhere = pl.BlockSpec(memory_space=pl.ANY)
    tile_shape = jax.ShapeDtypeStruct(queries.shape, jnp.bfloat16)
    piece = jax.ShapeDtypeStruct((2 * short, DH), jnp.bfloat16)
    spots_shape = jax.ShapeDtypeStruct((blocks_here, 3 + GLOB + RAND), jnp.int32)
    *pieces, spots, query_here, grad_here = pl.pallas_call(
        lambda *refs: pack_kernel(seq_count, head_count, *refs),
        in_specs=[anywhere] * 6,
        out_specs=[anywhere] * head_count + [smem] + [anywhere] * 2,
        out_shape=[piece] * head_count + [spots_shape, tile_shape, tile_shape],
        scratch_shapes=[
            pltpu.SMEM(rand_blocks.shape, jnp.int32),
            pltpu.SMEM(glob_blocks.shape, jnp.int32),
            pltpu.SemaphoreType.DMA((2 * head_count + 4,)),
        ],
        compiler_params=small_grant(),
    )(
        *[
            pltpu.with_memory_space_constraint(x, pltpu.HBM)
            for x in (rand_blocks, glob_blocks, keys, values, queries, d_out)
        ]
    )
    pieces = [pieces[0]] + [
        lax.ppermute(pieces[k], "head", flips(head_count, k)) for k in range(1, head_count)
    ]

    def along_far(own):
        parts = [own]
        for k in range(2, seq_count, 2):
            parts.append(lax.ppermute(own, "seq", flips(seq_count, k)))
        return parts

    def to_near(part):
        return lax.ppermute(part, "seq", flips(seq_count, 1))

    key_parts = along_far(jnp.stack([p[:short] for p in pieces]))
    key_parts += [to_near(p) for p in key_parts]
    value_parts = along_far(jnp.stack([p[short:] for p in pieces]))
    key_parts, value_parts = lax.optimization_barrier((key_parts, value_parts))
    value_parts.append(to_near(jnp.concatenate(value_parts)))

    tile = pl.BlockSpec((BLOCK, width), lambda i: (i, 0))
    square = pl.BlockSpec((1, listed, columns), lambda i: (i, 0, 0))
    listing = pl.BlockSpec((1, listed, DH), lambda i: (i, 0, 0))
    half = (pair_count, blocks_here, BLOCK, DH)
    whole = pl.BlockSpec(half, lambda i: (0, 0, 0, 0))
    square_shape = jax.ShapeDtypeStruct((blocks_here, listed, columns), jnp.bfloat16)
    listing_shape = jax.ShapeDtypeStruct((blocks_here, listed, DH), jnp.bfloat16)
    keep_shape = jax.ShapeDtypeStruct(half, jnp.float32)
    ship_shape = jax.ShapeDtypeStruct(half, jnp.bfloat16)
    library = pltpu.VMEM((seq_count * blocks_here, BLOCK, DH), jnp.bfloat16)
    total = pltpu.VMEM((seq_count * blocks_here, BLOCK, DH), jnp.float32)
    sems = pltpu.SemaphoreType.DMA((seq_count,))

    probs, key_lists, value_keep, value_ship = pl.pallas_call(
        lambda *refs: probs_kernel(seq_count, size, *refs),
        grid=(blocks_here,),
        in_specs=[smem, tile, tile] + [anywhere] * len(key_parts),
        out_specs=[square, listing, whole, whole],
        out_shape=[square_shape, listing_shape, keep_shape, ship_shape],
        scratch_shapes=[library, total, sems],
        **kernel_options(2, pairs),
    )(spots, query_here, grad_here, *key_parts)
    value_near = lax.ppermute(value_ship, "seq", flips(seq_count, 1))
    attn_out, dscores, key_keep, key_ship = pl.pallas_call(
        lambda *refs: dscores_kernel(size, *refs),
        grid=(blocks_here,),
        in_specs=[smem, tile, tile, square] + [anywhere] * len(value_parts),
        out_specs=[tile, square, whole, whole],
        out_shape=[tile_shape, square_shape, keep_shape, ship_shape],
        scratch_shapes=[library, total, pltpu.VMEM((listed, DH), jnp.bfloat16), sems],
        **kernel_options(3, pairs),
    )(spots, query_here, grad_here, probs, *value_parts)
    key_near = lax.ppermute(key_ship, "seq", flips(seq_count, 1))
    d_queries = pl.pallas_call(
        lambda *refs: dquery_kernel(size, *refs),
        grid=(blocks_here,),
        in_specs=[square, listing],
        out_specs=tile,
        out_shape=tile_shape,
        **kernel_options(1, pairs),
    )(dscores, key_lists)

    key_near, d_queries = lax.optimization_barrier((key_near, d_queries))

    def returned(keep, near):
        sums = keep + near.astype(jnp.float32)
        result = sums[0]
        for pair in range(pair_count - 1, 0, -1):
            result = result + lax.ppermute(
                sums[pair].astype(jnp.bfloat16), "seq", flips(seq_count, 2 * pair)
            ).astype(jnp.float32)
        return result

    packed = jnp.concatenate(
        [returned(key_keep, key_near), returned(value_keep, value_near)], axis=1
    ).astype(jnp.bfloat16)
    back = [packed[0]] + [
        lax.ppermute(packed[k], "head", flips(head_count, k)) for k in range(1, head_count)
    ]
    flat = jax.ShapeDtypeStruct(keys.shape, jnp.bfloat16)
    d_keys, d_values = pl.pallas_call(
        unpack_kernel, out_shape=[flat, flat], compiler_params=small_grant()
    )(*back)
    return (attn_out, d_queries, d_keys, d_values)


def body(queries, keys, values, d_out, rand_blocks, glob_blocks):
    seq_count = lax.axis_size("seq")
    head_count = lax.axis_size("head")
    blocks_here = rand_blocks.shape[0]
    capacity = -(-rand_blocks.size // seq_count)
    powers = all(n & (n - 1) == 0 for n in (seq_count, head_count))
    fits = keys.shape[0] == BLOCK and blocks_here == head_count
    if capacity >= blocks_here and seq_count > 1 and powers and fits:
        return whole_body(queries, keys, values, d_out, rand_blocks, glob_blocks)
    return request_body(queries, keys, values, d_out, rand_blocks, glob_blocks)


def solution(mesh):
    in_specs = (
        P("seq", "head"),
        P(("seq", "head"), None),
        P(("seq", "head"), None),
        P("seq", "head"),
        P("seq", None),
        P(),
    )
    out_specs = (
        P("seq", "head"),
        P("seq", "head"),
        P(("seq", "head"), None),
        P(("seq", "head"), None),
    )
    return jax.shard_map(body, mesh=mesh, in_specs=in_specs, out_specs=out_specs, check_vma=False)
```

```python
import math

import jax
import jax.numpy as jnp
from jax import lax
from jax.experimental import pallas as pl
from jax.experimental.pallas import tpu as pltpu
from jax.sharding import PartitionSpec as P

DH = 128
KVH = 4
BLOCK = 64
GLOB = 2
RAND = 8


NEG_FILL = -1e30


def padded_2(cells, sides, width):
    for axis, dim in sides:
        count = lax.axis_size(axis)
        ends = count - 1
        head = lax.slice_in_dim(cells, 0, width, axis=dim)
        tail = lax.slice_in_dim(cells, cells.shape[dim] - width, cells.shape[dim], axis=dim)
        cells = jnp.concatenate(
            [
                lax.ppermute(tail, axis, [(i, (i + 1) % count) for i in range(ends)]),
                cells,
                lax.ppermute(head, axis, [((i + 1) % count, i) for i in range(ends)]),
            ],
            axis=dim,
        )
    return cells


def broadcast(block, axis, source):
    block = jnp.where(lax.axis_index(axis) == source, block, jnp.zeros_like(block))
    return lax.psum(block, axis)


def key_rows(library, spots):
    chosen = jnp.stack(
        [
            lax.dynamic_index_in_dim(library, spots[i], 0, keepdims=False)
            for i in range(spots.shape[0])
        ]
    )
    flat = chosen.reshape(chosen.shape[0] * chosen.shape[1], chosen.shape[2])
    return (flat[:, :DH], flat[:, DH:])


def masked_scores(query_block, keys_here, allowed_row):
    factor = DH ** (-0.5)
    scores = (
        jnp.einsum("thd,kd->htk", query_block, keys_here, preferred_element_type=jnp.float32)
        * factor
    )
    widened = jnp.repeat(allowed_row, keys_here.shape[0] // allowed_row.shape[0])
    return jnp.where(widened[None, None, :], scores, NEG_FILL)


def request_body(queries, keys, values, d_out, rand_blocks, glob_blocks):
    seq_count = lax.axis_size("seq")
    here = lax.axis_index("seq")
    short = keys.shape[0]
    stacked = jnp.concatenate(
        [keys.reshape(short, KVH, DH), values.reshape(short, KVH, DH)], axis=2
    )
    mine = lax.all_to_all(stacked, "head", split_axis=1, concat_axis=0, tiled=True)
    tok_count = mine.shape[0]
    blocks_here = tok_count // BLOCK
    flat_pairs = mine.reshape(tok_count, 2 * DH)
    own_blocks = flat_pairs.reshape(blocks_here, BLOCK, 2 * DH)
    padded = padded_2(flat_pairs, (("seq", 0),), BLOCK)
    window = padded.reshape(blocks_here + 2, BLOCK, 2 * DH)
    global_parts = []
    for number in range(GLOB):
        target = glob_blocks[number]
        piece = lax.dynamic_index_in_dim(own_blocks, target % blocks_here, 0, keepdims=False)
        global_parts.append(broadcast(piece, "seq", target // blocks_here))
    global_pairs = jnp.stack(global_parts)
    entries = rand_blocks.reshape(-1)
    entry_count = entries.shape[0]
    capacity = -(-entry_count // seq_count)
    position_count = seq_count * capacity
    owners = entries // blocks_here
    inner_index = entries % blocks_here
    order = jnp.arange(entry_count, dtype=jnp.int32)
    earlier = (owners[:, None] == owners[None, :]) & (order[:, None] > order[None, :])
    ranks = jnp.sum(earlier.astype(jnp.int32), axis=1)
    slots = owners * capacity + ranks
    placing = slots[None, :] == jnp.arange(position_count, dtype=jnp.int32)[:, None]
    wanted = jnp.sum(jnp.where(placing, inner_index[None, :], 0), axis=1).reshape(
        seq_count, capacity
    )
    incoming = lax.all_to_all(wanted, "seq", split_axis=0, concat_axis=0, tiled=True).reshape(
        position_count
    )
    block_ids = jnp.arange(blocks_here, dtype=jnp.int32)
    picking = (incoming[:, None] == block_ids[None, :]).astype(jnp.bfloat16)
    served = (
        jnp.dot(
            picking,
            own_blocks.reshape(blocks_here, BLOCK * 2 * DH),
            preferred_element_type=jnp.float32,
        )
        .astype(jnp.bfloat16)
        .reshape(seq_count, capacity, BLOCK, 2 * DH)
    )
    fetched = lax.all_to_all(served, "seq", split_axis=0, concat_axis=0, tiled=True).reshape(
        position_count, BLOCK, 2 * DH
    )
    window_ids = jnp.stack([block_ids, block_ids + 1, block_ids + 2], axis=1)
    global_ids = jnp.broadcast_to(
        blocks_here + 2 + jnp.arange(GLOB, dtype=jnp.int32), (blocks_here, GLOB)
    )
    random_ids = blocks_here + 2 + GLOB + slots.reshape(blocks_here, RAND)
    positions = jnp.concatenate([window_ids, global_ids, random_ids], axis=1)
    allowed = jnp.concatenate(
        [
            jnp.logical_not((block_ids == 0) & (here == 0))[:, None],
            jnp.ones((blocks_here, 1), jnp.bool_),
            jnp.logical_not((block_ids == blocks_here - 1) & (here == seq_count - 1))[:, None],
            jnp.ones((blocks_here, GLOB + RAND), jnp.bool_),
        ],
        axis=1,
    )
    library = jnp.concatenate([window, global_pairs, fetched], axis=0)
    heads_here = queries.shape[1] // DH
    query_blocks = queries.reshape(blocks_here, BLOCK, heads_here, DH)
    grad_blocks = d_out.reshape(blocks_here, BLOCK, heads_here, DH)

    def forward_step(inputs):
        query_block, spots, allowed_row = inputs
        keys_here, values_here = key_rows(library, spots)
        scores = masked_scores(query_block, keys_here, allowed_row)
        peak = jnp.max(scores, axis=-1, keepdims=True)
        logsum = peak + jnp.log(jnp.sum(jnp.exp(scores - peak), axis=-1, keepdims=True))
        probs16 = jnp.exp(scores - logsum).astype(jnp.bfloat16)
        result = jnp.einsum("htk,kd->thd", probs16, values_here, preferred_element_type=jnp.float32)
        return (result.astype(jnp.bfloat16), logsum)

    out_blocks, logsums = lax.map(forward_step, (query_blocks, positions, allowed))
    refetched = lax.all_to_all(served, "seq", split_axis=0, concat_axis=0, tiled=True).reshape(
        position_count, BLOCK, 2 * DH
    )
    library_back = jnp.concatenate([window, global_pairs, refetched], axis=0)

    def backward_step(inputs):
        query_block, gradient_tile, out_block, logsum, spots, allowed_row = inputs
        keys_here, values_here = key_rows(library_back, spots)
        factor = DH ** (-0.5)
        scores = masked_scores(query_block, keys_here, allowed_row)
        probs = jnp.exp(scores - logsum)
        probs16 = probs.astype(jnp.bfloat16)
        delta = jnp.sum(gradient_tile.astype(jnp.float32) * out_block.astype(jnp.float32), axis=-1)
        dprobs = jnp.einsum(
            "thd,kd->htk", gradient_tile, values_here, preferred_element_type=jnp.float32
        )
        dscores = (probs * (dprobs - jnp.transpose(delta)[:, :, None])).astype(jnp.bfloat16)
        dquery = (
            jnp.einsum("htk,kd->thd", dscores, keys_here, preferred_element_type=jnp.float32)
            * factor
        )
        dkey = (
            jnp.einsum("htk,thd->kd", dscores, query_block, preferred_element_type=jnp.float32)
            * factor
        )
        dvalue = jnp.einsum(
            "htk,thd->kd", probs16, gradient_tile, preferred_element_type=jnp.float32
        )
        terms = jnp.concatenate([dkey, dvalue], axis=1).reshape(spots.shape[0], BLOCK, 2 * DH)
        return (dquery.astype(jnp.bfloat16), terms)

    dquery_blocks, terms = lax.map(
        backward_step, (query_blocks, grad_blocks, out_blocks, logsums, positions, allowed)
    )
    attn_out = out_blocks.reshape(tok_count, heads_here * DH)
    d_queries = dquery_blocks.reshape(tok_count, heads_here * DH)
    prev_terms = terms[:, 0]
    self_terms = terms[:, 1]
    next_terms = terms[:, 2]
    zero_block = jnp.zeros((1, BLOCK, 2 * DH), jnp.float32)
    grads = (
        self_terms
        + jnp.concatenate([prev_terms[1:], zero_block], axis=0)
        + jnp.concatenate([zero_block, next_terms[:-1]], axis=0)
    )
    rims = jnp.concatenate([prev_terms[0], next_terms[-1]], axis=0).astype(jnp.bfloat16)
    arrived = padded_2(rims, (("seq", 0),), BLOCK)
    from_left = arrived[:BLOCK].astype(jnp.float32)
    from_right = arrived[3 * BLOCK :].astype(jnp.float32)
    edge_first = jnp.concatenate(
        [from_left[None], jnp.zeros((blocks_here - 1, BLOCK, 2 * DH), jnp.float32)], axis=0
    )
    edge_last = jnp.concatenate(
        [jnp.zeros((blocks_here - 1, BLOCK, 2 * DH), jnp.float32), from_right[None]], axis=0
    )
    grads = grads + edge_first + edge_last
    global_terms = jnp.sum(terms[:, 3 : 3 + GLOB], axis=0)
    global_total = lax.psum(global_terms, "seq")
    global_hits = ((glob_blocks // blocks_here)[:, None] == here) & (
        (glob_blocks % blocks_here)[:, None] == block_ids[None, :]
    )
    grads = grads + jnp.sum(
        jnp.where(global_hits[:, :, None, None], global_total[:, None], 0.0), axis=0
    )
    random_terms = terms[:, 3 + GLOB :].reshape(entry_count, BLOCK * 2 * DH).astype(jnp.bfloat16)
    outgoing = jnp.dot(
        placing.astype(jnp.bfloat16), random_terms, preferred_element_type=jnp.float32
    ).astype(jnp.bfloat16)
    returned = lax.all_to_all(
        outgoing.reshape(seq_count, capacity, BLOCK, 2 * DH),
        "seq",
        split_axis=0,
        concat_axis=0,
        tiled=True,
    )
    landing = (incoming[None, :] == block_ids[:, None]).astype(jnp.bfloat16)
    grads = grads + jnp.dot(
        landing,
        returned.reshape(position_count, BLOCK * 2 * DH),
        preferred_element_type=jnp.float32,
    ).reshape(blocks_here, BLOCK, 2 * DH)
    packed = grads.astype(jnp.bfloat16).reshape(tok_count, 1, 2 * DH)
    restored = lax.all_to_all(packed, "head", split_axis=0, concat_axis=1, tiled=True)
    d_keys = restored[:, :, :DH].reshape(short, KVH * DH)
    d_values = restored[:, :, DH:].reshape(short, KVH * DH)
    return (attn_out, d_queries, d_keys, d_values)


def flips(count, bits):
    return [(i, i ^ bits) for i in range(count)]


def head_columns(head, offset):
    return pl.ds(pl.multiple_of((head ^ offset) * DH, DH), DH)


def pack_kernel(seq_count, head_count, *refs):
    rand_from, glob_from, keys_ref, values_ref, query_ref, grad_ref = refs[:6]
    piece_refs = refs[6 : 6 + head_count]
    spots_ref, query_out, grad_out, rand_ref, glob_ref, sems = refs[6 + head_count :]
    here = lax.axis_index("seq")
    head = lax.axis_index("head")
    short = keys_ref.shape[0]
    copies = [(rand_from, rand_ref), (glob_from, glob_ref)]
    for offset, piece in enumerate(piece_refs):
        columns = head_columns(head, offset)
        copies.append((keys_ref.at[:, columns], piece.at[pl.ds(0, short)]))
        copies.append((values_ref.at[:, columns], piece.at[pl.ds(short, short)]))
    copies += [(query_ref, query_out), (grad_ref, grad_out)]
    copies = [pltpu.make_async_copy(a, b, sems.at[n]) for n, (a, b) in enumerate(copies)]
    for copy in copies:
        copy.start()
    copies[0].wait()
    copies[1].wait()
    blocks_here = rand_ref.shape[0]
    last = seq_count * blocks_here - 1
    for step in range(blocks_here):
        block = here * blocks_here + step
        names = [jnp.maximum(block - 1, 0), block, jnp.minimum(block + 1, last)]
        names += [glob_ref[i] for i in range(GLOB)]
        names += [rand_ref[step, i] for i in range(RAND)]
        for number, name in enumerate(names):
            owner = lax.div(name, blocks_here) ^ here
            spots_ref[step, number] = owner * blocks_here + (lax.rem(name, blocks_here) ^ head)
    for copy in copies[2:]:
        copy.wait()


def unpack_kernel(*refs):
    piece_refs, (keys_ref, values_ref) = refs[:-2], refs[-2:]
    head = lax.axis_index("head")
    short = keys_ref.shape[0]
    for offset, piece in enumerate(piece_refs):
        columns = head_columns(head, offset)
        keys_ref[:, columns] = piece[:short, :]
        values_ref[:, columns] = piece[short:, :]


def dot(left, right, left_dim, right_dim):
    return lax.dot_general(
        left,
        right,
        (((left_dim,), (right_dim,)), ((), ())),
        preferred_element_type=jnp.float32,
    )


def load_parts(part_refs, library, sems):
    copies, at = [], 0
    for part in part_refs:
        size = part.shape[0]
        copies.append(
            pltpu.make_async_copy(part, library.at[pl.ds(at, size)], sems.at[len(copies)])
        )
        at += size
    return copies


def listed_spots(spots_ref, step):
    return [spots_ref[step, number] for number in range(spots_ref.shape[1])]


def begin(step, part_refs, library, total, sems):
    @pl.when(step == 0)
    def _():
        copies = load_parts(part_refs, library, sems)
        for copy in copies:
            copy.start()
        total[...] = jnp.zeros_like(total)
        for copy in copies:
            copy.wait()


def add_terms(total, spots, terms):
    for number, spot in enumerate(spots):
        total[spot] += terms[number * BLOCK : (number + 1) * BLOCK]


def finish(step, total, keep_ref, ship_ref):
    pairs, size = keep_ref.shape[:2]

    @pl.when(step == pl.num_programs(0) - 1)
    def _():
        for pair in range(pairs):
            keep_ref[pair] = total[pl.ds(2 * pair * size, size)]
            ship_ref[pair] = total[pl.ds((2 * pair + 1) * size, size)].astype(jnp.bfloat16)


def stacked_heads(ref, chunk):
    return jnp.concatenate([ref[:, h * DH : (h + 1) * DH] for h in chunk], axis=0)


def chunks_of(heads, size):
    return [range(start, start + size) for start in range(0, heads, size)]


def probs_kernel(seq_count, size, *refs):
    spots_ref, query_ref, grad_ref = refs[:3]
    part_refs = refs[3 : 3 + seq_count]
    probs_ref, rows_ref, keep_ref, ship_ref, library, total, sems = refs[3 + seq_count :]
    blocks_here = part_refs[0].shape[0]
    all_blocks = seq_count * blocks_here
    step = pl.program_id(0)
    begin(step, part_refs, library, total, sems)
    block = lax.axis_index("seq") * blocks_here + step
    spots = listed_spots(spots_ref, step)
    for number, spot in enumerate(spots):
        rows_ref[0, pl.ds(number * BLOCK, BLOCK), :] = library[spot]
    first_bias = jnp.where(block == 0, NEG_FILL, 0.0)
    last_bias = jnp.where(block == all_blocks - 1, NEG_FILL, 0.0)
    scale = DH ** (-0.5) * math.log2(math.e)
    terms = 0.0
    for chunk in chunks_of(query_ref.shape[1] // DH, size):
        query = stacked_heads(query_ref, chunk)
        grad = stacked_heads(grad_ref, chunk)
        scores = dot(rows_ref[0], query, 1, 1)
        scores = jnp.concatenate(
            [
                scores[:BLOCK] + first_bias,
                scores[BLOCK : 2 * BLOCK],
                scores[2 * BLOCK : 3 * BLOCK] + last_bias,
                scores[3 * BLOCK :],
            ],
            axis=0,
        )
        peak = jnp.max(scores, axis=0, keepdims=True)
        weights = jnp.exp2((scores - peak) * scale)
        probs = weights * (1.0 / jnp.sum(weights, axis=0, keepdims=True))
        probs16 = probs.astype(jnp.bfloat16)
        probs_ref[0, :, chunk[0] * BLOCK : (chunk[-1] + 1) * BLOCK] = probs16
        terms = terms + dot(probs16, grad, 1, 0)
    add_terms(total, spots, terms)
    finish(step, total, keep_ref, ship_ref)


def dscores_kernel(size, *refs):
    spots_ref, query_ref, grad_ref, probs_ref = refs[:4]
    part_refs, refs = refs[4:-8], refs[-8:]
    out_ref, dscores_ref, keep_ref, ship_ref, library, total, rows_ref, sems = refs
    step = pl.program_id(0)
    begin(step, part_refs, library, total, sems)
    spots = listed_spots(spots_ref, step)
    for number, spot in enumerate(spots):
        rows_ref[pl.ds(number * BLOCK, BLOCK), :] = library[spot]
    terms = 0.0
    for chunk in chunks_of(query_ref.shape[1] // DH, size):
        columns = slice(chunk[0] * BLOCK, (chunk[-1] + 1) * BLOCK)
        query = stacked_heads(query_ref, chunk)
        grad = stacked_heads(grad_ref, chunk)
        probs16 = probs_ref[0, :, columns]
        result = dot(rows_ref[...], probs16, 0, 0).astype(jnp.bfloat16).astype(jnp.float32)
        grad_across = jnp.transpose(grad.astype(jnp.float32))
        delta = jnp.sum(grad_across * result, axis=0, keepdims=True)
        dprobs = dot(rows_ref[...], grad, 1, 1)
        dscores = (probs16.astype(jnp.float32) * (dprobs - delta)).astype(jnp.bfloat16)
        dscores_ref[0, :, columns] = dscores
        terms = terms + dot(dscores, query, 1, 0)
        down = jnp.transpose(result).astype(jnp.bfloat16)
        for number, h in enumerate(chunk):
            out_ref[:, h * DH : (h + 1) * DH] = down[number * BLOCK : (number + 1) * BLOCK]
    add_terms(total, spots, terms * DH ** (-0.5))
    finish(step, total, keep_ref, ship_ref)


def dquery_kernel(size, dscores_ref, rows_ref, dquery_ref):
    for chunk in chunks_of(dquery_ref.shape[1] // DH, size):
        columns = slice(chunk[0] * BLOCK, (chunk[-1] + 1) * BLOCK)
        across = dot(rows_ref[0], dscores_ref[0, :, columns], 0, 0) * DH ** (-0.5)
        down = jnp.transpose(across).astype(jnp.bfloat16)
        for number, h in enumerate(chunk):
            dquery_ref[:, h * DH : (h + 1) * DH] = down[number * BLOCK : (number + 1) * BLOCK]


def small_grant():
    return pltpu.CompilerParams(vmem_limit_bytes=8 * 1024 * 1024)


def kernel_options(products, pairs):
    return {
        "compiler_params": pltpu.CompilerParams(vmem_limit_bytes=40 * 1024 * 1024),
        "cost_estimate": pl.CostEstimate(
            flops=4 * products * pairs * DH, bytes_accessed=4 * pairs, transcendentals=pairs
        ),
    }


def whole_body(queries, keys, values, d_out, rand_blocks, glob_blocks):
    seq_count = lax.axis_size("seq")
    head_count = lax.axis_size("head")
    short = keys.shape[0]
    tok_count, width = queries.shape
    heads_here = width // DH
    blocks_here = tok_count // BLOCK
    pair_count = seq_count // 2
    listed = (3 + GLOB + RAND) * BLOCK
    columns = heads_here * BLOCK
    pairs = blocks_here * listed * columns
    size = heads_here

    smem = pl.BlockSpec(memory_space=pltpu.SMEM)
    anywhere = pl.BlockSpec(memory_space=pl.ANY)
    tile_shape = jax.ShapeDtypeStruct(queries.shape, jnp.bfloat16)
    piece = jax.ShapeDtypeStruct((2 * short, DH), jnp.bfloat16)
    spots_shape = jax.ShapeDtypeStruct((blocks_here, 3 + GLOB + RAND), jnp.int32)
    *pieces, spots, query_here, grad_here = pl.pallas_call(
        lambda *refs: pack_kernel(seq_count, head_count, *refs),
        in_specs=[anywhere] * 6,
        out_specs=[anywhere] * head_count + [smem] + [anywhere] * 2,
        out_shape=[piece] * head_count + [spots_shape, tile_shape, tile_shape],
        scratch_shapes=[
            pltpu.SMEM(rand_blocks.shape, jnp.int32),
            pltpu.SMEM(glob_blocks.shape, jnp.int32),
            pltpu.SemaphoreType.DMA((2 * head_count + 4,)),
        ],
        compiler_params=small_grant(),
    )(
        *[
            pltpu.with_memory_space_constraint(x, pltpu.HBM)
            for x in (rand_blocks, glob_blocks, keys, values, queries, d_out)
        ]
    )
    pieces = [pieces[0]] + [
        lax.ppermute(pieces[k], "head", flips(head_count, k)) for k in range(1, head_count)
    ]

    def along_far(own):
        parts = [own]
        for k in range(2, seq_count, 2):
            parts.append(lax.ppermute(own, "seq", flips(seq_count, k)))
        return parts

    def to_near(part):
        return lax.ppermute(part, "seq", flips(seq_count, 1))

    key_far = along_far(jnp.stack([p[:short] for p in pieces]))
    key_parts = [part for far in key_far for part in (far, to_near(far))]
    value_own = jnp.stack([p[short:] for p in pieces])
    value_pair = jnp.concatenate([value_own, to_near(value_own)])
    value_pair, _ = lax.optimization_barrier((value_pair, key_far[1:]))
    value_parts = along_far(value_pair)

    tile = pl.BlockSpec((BLOCK, width), lambda i: (i, 0))
    square = pl.BlockSpec((1, listed, columns), lambda i: (i, 0, 0))
    listing = pl.BlockSpec((1, listed, DH), lambda i: (i, 0, 0))
    half = (pair_count, blocks_here, BLOCK, DH)
    whole = pl.BlockSpec(half, lambda i: (0, 0, 0, 0))
    square_shape = jax.ShapeDtypeStruct((blocks_here, listed, columns), jnp.bfloat16)
    listing_shape = jax.ShapeDtypeStruct((blocks_here, listed, DH), jnp.bfloat16)
    keep_shape = jax.ShapeDtypeStruct(half, jnp.float32)
    ship_shape = jax.ShapeDtypeStruct(half, jnp.bfloat16)
    library = pltpu.VMEM((seq_count * blocks_here, BLOCK, DH), jnp.bfloat16)
    total = pltpu.VMEM((seq_count * blocks_here, BLOCK, DH), jnp.float32)
    sems = pltpu.SemaphoreType.DMA((seq_count,))

    probs, key_lists, value_keep, value_ship = pl.pallas_call(
        lambda *refs: probs_kernel(seq_count, size, *refs),
        grid=(blocks_here,),
        in_specs=[smem, tile, tile] + [anywhere] * len(key_parts),
        out_specs=[square, listing, whole, whole],
        out_shape=[square_shape, listing_shape, keep_shape, ship_shape],
        scratch_shapes=[library, total, sems],
        **kernel_options(2, pairs),
    )(spots, query_here, grad_here, *key_parts)
    value_near = lax.ppermute(value_ship, "seq", flips(seq_count, 1))
    attn_out, dscores, key_keep, key_ship = pl.pallas_call(
        lambda *refs: dscores_kernel(size, *refs),
        grid=(blocks_here,),
        in_specs=[smem, tile, tile, square] + [anywhere] * len(value_parts),
        out_specs=[tile, square, whole, whole],
        out_shape=[tile_shape, square_shape, keep_shape, ship_shape],
        scratch_shapes=[library, total, pltpu.VMEM((listed, DH), jnp.bfloat16), sems],
        **kernel_options(3, pairs),
    )(spots, query_here, grad_here, probs, *value_parts)
    key_near = lax.ppermute(key_ship, "seq", flips(seq_count, 1))
    d_queries = pl.pallas_call(
        lambda *refs: dquery_kernel(size, *refs),
        grid=(blocks_here,),
        in_specs=[square, listing],
        out_specs=tile,
        out_shape=tile_shape,
        **kernel_options(1, pairs),
    )(*lax.optimization_barrier((dscores, key_lists, key_near))[:2])

    def returned(keep, near):
        sums = keep + near.astype(jnp.float32)
        result = sums[0]
        for pair in range(pair_count - 1, 0, -1):
            result = result + lax.ppermute(
                sums[pair].astype(jnp.bfloat16), "seq", flips(seq_count, 2 * pair)
            ).astype(jnp.float32)
        return result

    packed = jnp.concatenate(
        [returned(key_keep, key_near), returned(value_keep, value_near)], axis=1
    ).astype(jnp.bfloat16)
    back = [packed[0]] + [
        lax.ppermute(packed[k], "head", flips(head_count, k)) for k in range(1, head_count)
    ]
    flat = jax.ShapeDtypeStruct(keys.shape, jnp.bfloat16)
    d_keys, d_values = pl.pallas_call(
        unpack_kernel, out_shape=[flat, flat], compiler_params=small_grant()
    )(*back)
    return (attn_out, d_queries, d_keys, d_values)


def body(queries, keys, values, d_out, rand_blocks, glob_blocks):
    seq_count = lax.axis_size("seq")
    head_count = lax.axis_size("head")
    blocks_here = rand_blocks.shape[0]
    capacity = -(-rand_blocks.size // seq_count)
    powers = all(n & (n - 1) == 0 for n in (seq_count, head_count))
    fits = keys.shape[0] == BLOCK and blocks_here == head_count
    if capacity >= blocks_here and seq_count > 1 and powers and fits:
        return whole_body(queries, keys, values, d_out, rand_blocks, glob_blocks)
    return request_body(queries, keys, values, d_out, rand_blocks, glob_blocks)


def solution(mesh):
    in_specs = (
        P("seq", "head"),
        P(("seq", "head"), None),
        P(("seq", "head"), None),
        P("seq", "head"),
        P("seq", None),
        P(),
    )
    out_specs = (
        P("seq", "head"),
        P("seq", "head"),
        P(("seq", "head"), None),
        P(("seq", "head"), None),
    )
    return jax.shard_map(body, mesh=mesh, in_specs=in_specs, out_specs=out_specs, check_vma=False)
```

```python
import math

import jax
import jax.numpy as jnp
from jax import lax
from jax.experimental import pallas as pl
from jax.experimental.pallas import tpu as pltpu
from jax.sharding import PartitionSpec as P

DH = 128
KVH = 4
BLOCK = 64
GLOB = 2
RAND = 8


NEG_FILL = -1e30


def padded_2(cells, sides, width):
    for axis, dim in sides:
        count = lax.axis_size(axis)
        ends = count - 1
        head = lax.slice_in_dim(cells, 0, width, axis=dim)
        tail = lax.slice_in_dim(cells, cells.shape[dim] - width, cells.shape[dim], axis=dim)
        cells = jnp.concatenate(
            [
                lax.ppermute(tail, axis, [(i, (i + 1) % count) for i in range(ends)]),
                cells,
                lax.ppermute(head, axis, [((i + 1) % count, i) for i in range(ends)]),
            ],
            axis=dim,
        )
    return cells


def broadcast(block, axis, source):
    block = jnp.where(lax.axis_index(axis) == source, block, jnp.zeros_like(block))
    return lax.psum(block, axis)


def key_rows(library, spots):
    chosen = jnp.stack(
        [
            lax.dynamic_index_in_dim(library, spots[i], 0, keepdims=False)
            for i in range(spots.shape[0])
        ]
    )
    flat = chosen.reshape(chosen.shape[0] * chosen.shape[1], chosen.shape[2])
    return (flat[:, :DH], flat[:, DH:])


def masked_scores(query_block, keys_here, allowed_row):
    factor = DH ** (-0.5)
    scores = (
        jnp.einsum("thd,kd->htk", query_block, keys_here, preferred_element_type=jnp.float32)
        * factor
    )
    widened = jnp.repeat(allowed_row, keys_here.shape[0] // allowed_row.shape[0])
    return jnp.where(widened[None, None, :], scores, NEG_FILL)


def request_body(queries, keys, values, d_out, rand_blocks, glob_blocks):
    seq_count = lax.axis_size("seq")
    here = lax.axis_index("seq")
    short = keys.shape[0]
    stacked = jnp.concatenate(
        [keys.reshape(short, KVH, DH), values.reshape(short, KVH, DH)], axis=2
    )
    mine = lax.all_to_all(stacked, "head", split_axis=1, concat_axis=0, tiled=True)
    tok_count = mine.shape[0]
    blocks_here = tok_count // BLOCK
    flat_pairs = mine.reshape(tok_count, 2 * DH)
    own_blocks = flat_pairs.reshape(blocks_here, BLOCK, 2 * DH)
    padded = padded_2(flat_pairs, (("seq", 0),), BLOCK)
    window = padded.reshape(blocks_here + 2, BLOCK, 2 * DH)
    global_parts = []
    for number in range(GLOB):
        target = glob_blocks[number]
        piece = lax.dynamic_index_in_dim(own_blocks, target % blocks_here, 0, keepdims=False)
        global_parts.append(broadcast(piece, "seq", target // blocks_here))
    global_pairs = jnp.stack(global_parts)
    entries = rand_blocks.reshape(-1)
    entry_count = entries.shape[0]
    capacity = -(-entry_count // seq_count)
    position_count = seq_count * capacity
    owners = entries // blocks_here
    inner_index = entries % blocks_here
    order = jnp.arange(entry_count, dtype=jnp.int32)
    earlier = (owners[:, None] == owners[None, :]) & (order[:, None] > order[None, :])
    ranks = jnp.sum(earlier.astype(jnp.int32), axis=1)
    slots = owners * capacity + ranks
    placing = slots[None, :] == jnp.arange(position_count, dtype=jnp.int32)[:, None]
    wanted = jnp.sum(jnp.where(placing, inner_index[None, :], 0), axis=1).reshape(
        seq_count, capacity
    )
    incoming = lax.all_to_all(wanted, "seq", split_axis=0, concat_axis=0, tiled=True).reshape(
        position_count
    )
    block_ids = jnp.arange(blocks_here, dtype=jnp.int32)
    picking = (incoming[:, None] == block_ids[None, :]).astype(jnp.bfloat16)
    served = (
        jnp.dot(
            picking,
            own_blocks.reshape(blocks_here, BLOCK * 2 * DH),
            preferred_element_type=jnp.float32,
        )
        .astype(jnp.bfloat16)
        .reshape(seq_count, capacity, BLOCK, 2 * DH)
    )
    fetched = lax.all_to_all(served, "seq", split_axis=0, concat_axis=0, tiled=True).reshape(
        position_count, BLOCK, 2 * DH
    )
    window_ids = jnp.stack([block_ids, block_ids + 1, block_ids + 2], axis=1)
    global_ids = jnp.broadcast_to(
        blocks_here + 2 + jnp.arange(GLOB, dtype=jnp.int32), (blocks_here, GLOB)
    )
    random_ids = blocks_here + 2 + GLOB + slots.reshape(blocks_here, RAND)
    positions = jnp.concatenate([window_ids, global_ids, random_ids], axis=1)
    allowed = jnp.concatenate(
        [
            jnp.logical_not((block_ids == 0) & (here == 0))[:, None],
            jnp.ones((blocks_here, 1), jnp.bool_),
            jnp.logical_not((block_ids == blocks_here - 1) & (here == seq_count - 1))[:, None],
            jnp.ones((blocks_here, GLOB + RAND), jnp.bool_),
        ],
        axis=1,
    )
    library = jnp.concatenate([window, global_pairs, fetched], axis=0)
    heads_here = queries.shape[1] // DH
    query_blocks = queries.reshape(blocks_here, BLOCK, heads_here, DH)
    grad_blocks = d_out.reshape(blocks_here, BLOCK, heads_here, DH)

    def forward_step(inputs):
        query_block, spots, allowed_row = inputs
        keys_here, values_here = key_rows(library, spots)
        scores = masked_scores(query_block, keys_here, allowed_row)
        peak = jnp.max(scores, axis=-1, keepdims=True)
        logsum = peak + jnp.log(jnp.sum(jnp.exp(scores - peak), axis=-1, keepdims=True))
        probs16 = jnp.exp(scores - logsum).astype(jnp.bfloat16)
        result = jnp.einsum("htk,kd->thd", probs16, values_here, preferred_element_type=jnp.float32)
        return (result.astype(jnp.bfloat16), logsum)

    out_blocks, logsums = lax.map(forward_step, (query_blocks, positions, allowed))
    refetched = lax.all_to_all(served, "seq", split_axis=0, concat_axis=0, tiled=True).reshape(
        position_count, BLOCK, 2 * DH
    )
    library_back = jnp.concatenate([window, global_pairs, refetched], axis=0)

    def backward_step(inputs):
        query_block, gradient_tile, out_block, logsum, spots, allowed_row = inputs
        keys_here, values_here = key_rows(library_back, spots)
        factor = DH ** (-0.5)
        scores = masked_scores(query_block, keys_here, allowed_row)
        probs = jnp.exp(scores - logsum)
        probs16 = probs.astype(jnp.bfloat16)
        delta = jnp.sum(gradient_tile.astype(jnp.float32) * out_block.astype(jnp.float32), axis=-1)
        dprobs = jnp.einsum(
            "thd,kd->htk", gradient_tile, values_here, preferred_element_type=jnp.float32
        )
        dscores = (probs * (dprobs - jnp.transpose(delta)[:, :, None])).astype(jnp.bfloat16)
        dquery = (
            jnp.einsum("htk,kd->thd", dscores, keys_here, preferred_element_type=jnp.float32)
            * factor
        )
        dkey = (
            jnp.einsum("htk,thd->kd", dscores, query_block, preferred_element_type=jnp.float32)
            * factor
        )
        dvalue = jnp.einsum(
            "htk,thd->kd", probs16, gradient_tile, preferred_element_type=jnp.float32
        )
        terms = jnp.concatenate([dkey, dvalue], axis=1).reshape(spots.shape[0], BLOCK, 2 * DH)
        return (dquery.astype(jnp.bfloat16), terms)

    dquery_blocks, terms = lax.map(
        backward_step, (query_blocks, grad_blocks, out_blocks, logsums, positions, allowed)
    )
    attn_out = out_blocks.reshape(tok_count, heads_here * DH)
    d_queries = dquery_blocks.reshape(tok_count, heads_here * DH)
    prev_terms = terms[:, 0]
    self_terms = terms[:, 1]
    next_terms = terms[:, 2]
    zero_block = jnp.zeros((1, BLOCK, 2 * DH), jnp.float32)
    grads = (
        self_terms
        + jnp.concatenate([prev_terms[1:], zero_block], axis=0)
        + jnp.concatenate([zero_block, next_terms[:-1]], axis=0)
    )
    rims = jnp.concatenate([prev_terms[0], next_terms[-1]], axis=0).astype(jnp.bfloat16)
    arrived = padded_2(rims, (("seq", 0),), BLOCK)
    from_left = arrived[:BLOCK].astype(jnp.float32)
    from_right = arrived[3 * BLOCK :].astype(jnp.float32)
    edge_first = jnp.concatenate(
        [from_left[None], jnp.zeros((blocks_here - 1, BLOCK, 2 * DH), jnp.float32)], axis=0
    )
    edge_last = jnp.concatenate(
        [jnp.zeros((blocks_here - 1, BLOCK, 2 * DH), jnp.float32), from_right[None]], axis=0
    )
    grads = grads + edge_first + edge_last
    global_terms = jnp.sum(terms[:, 3 : 3 + GLOB], axis=0)
    global_total = lax.psum(global_terms, "seq")
    global_hits = ((glob_blocks // blocks_here)[:, None] == here) & (
        (glob_blocks % blocks_here)[:, None] == block_ids[None, :]
    )
    grads = grads + jnp.sum(
        jnp.where(global_hits[:, :, None, None], global_total[:, None], 0.0), axis=0
    )
    random_terms = terms[:, 3 + GLOB :].reshape(entry_count, BLOCK * 2 * DH).astype(jnp.bfloat16)
    outgoing = jnp.dot(
        placing.astype(jnp.bfloat16), random_terms, preferred_element_type=jnp.float32
    ).astype(jnp.bfloat16)
    returned = lax.all_to_all(
        outgoing.reshape(seq_count, capacity, BLOCK, 2 * DH),
        "seq",
        split_axis=0,
        concat_axis=0,
        tiled=True,
    )
    landing = (incoming[None, :] == block_ids[:, None]).astype(jnp.bfloat16)
    grads = grads + jnp.dot(
        landing,
        returned.reshape(position_count, BLOCK * 2 * DH),
        preferred_element_type=jnp.float32,
    ).reshape(blocks_here, BLOCK, 2 * DH)
    packed = grads.astype(jnp.bfloat16).reshape(tok_count, 1, 2 * DH)
    restored = lax.all_to_all(packed, "head", split_axis=0, concat_axis=1, tiled=True)
    d_keys = restored[:, :, :DH].reshape(short, KVH * DH)
    d_values = restored[:, :, DH:].reshape(short, KVH * DH)
    return (attn_out, d_queries, d_keys, d_values)


def flips(count, bits):
    return [(i, i ^ bits) for i in range(count)]


def head_columns(head, offset):
    return pl.ds(pl.multiple_of((head ^ offset) * DH, DH), DH)


def run_copies(copies):
    for copy in copies:
        copy.start()
    for copy in copies:
        copy.wait()


def pack_kernel(*refs):
    keys_ref, values_ref, *piece_refs, sems = refs
    head = lax.axis_index("head")
    short = keys_ref.shape[0]
    moves = []
    for offset, piece in enumerate(piece_refs):
        columns = head_columns(head, offset)
        moves.append((keys_ref.at[:, columns], piece.at[pl.ds(0, short)]))
        moves.append((values_ref.at[:, columns], piece.at[pl.ds(short, short)]))
    run_copies([pltpu.make_async_copy(a, b, sems.at[n]) for n, (a, b) in enumerate(moves)])


def list_kernel(seq_count, *refs):
    rand_from, glob_from, query_from, grad_from = refs[:4]
    spots_ref, query_ref, grad_ref, rand_ref, glob_ref, sems = refs[4:]
    here = lax.axis_index("seq")
    head = lax.axis_index("head")
    moves = [(rand_from, rand_ref), (glob_from, glob_ref)]
    moves += [(query_from, query_ref), (grad_from, grad_ref)]
    copies = [pltpu.make_async_copy(a, b, sems.at[n]) for n, (a, b) in enumerate(moves)]
    for copy in copies:
        copy.start()
    copies[0].wait()
    copies[1].wait()
    blocks_here = rand_ref.shape[0]
    last = seq_count * blocks_here - 1
    for step in range(blocks_here):
        block = here * blocks_here + step
        names = [jnp.maximum(block - 1, 0), block, jnp.minimum(block + 1, last)]
        names += [glob_ref[i] for i in range(GLOB)]
        names += [rand_ref[step, i] for i in range(RAND)]
        for number, name in enumerate(names):
            owner = lax.div(name, blocks_here) ^ here
            spots_ref[step, number] = owner * blocks_here + (lax.rem(name, blocks_here) ^ head)
    copies[2].wait()
    copies[3].wait()


def unpack_kernel(*refs):
    piece_refs, (keys_ref, values_ref) = refs[:-2], refs[-2:]
    head = lax.axis_index("head")
    short = keys_ref.shape[0]
    for offset, piece in enumerate(piece_refs):
        columns = head_columns(head, offset)
        keys_ref[:, columns] = piece[:short, :]
        values_ref[:, columns] = piece[short:, :]


def dot(left, right, left_dim, right_dim):
    return lax.dot_general(
        left,
        right,
        (((left_dim,), (right_dim,)), ((), ())),
        preferred_element_type=jnp.float32,
    )


def load_parts(part_refs, library, sems):
    copies, at = [], 0
    for part in part_refs:
        size = part.shape[0]
        copies.append(
            pltpu.make_async_copy(part, library.at[pl.ds(at, size)], sems.at[len(copies)])
        )
        at += size
    return copies


def listed_spots(spots_ref, step):
    return [spots_ref[step, number] for number in range(spots_ref.shape[1])]


def begin(step, part_refs, library, total, sems):
    @pl.when(step == 0)
    def _():
        copies = load_parts(part_refs, library, sems)
        for copy in copies:
            copy.start()
        total[...] = jnp.zeros_like(total)
        for copy in copies:
            copy.wait()


def add_terms(total, spots, terms):
    for number, spot in enumerate(spots):
        total[spot] += terms[number * BLOCK : (number + 1) * BLOCK]


def finish(step, total, keep_ref, ship_ref):
    pairs, size = keep_ref.shape[:2]

    @pl.when(step == pl.num_programs(0) - 1)
    def _():
        for pair in range(pairs):
            keep_ref[pair] = total[pl.ds(2 * pair * size, size)]
            ship_ref[pair] = total[pl.ds((2 * pair + 1) * size, size)].astype(jnp.bfloat16)


def stacked_heads(ref, chunk):
    return jnp.concatenate([ref[:, h * DH : (h + 1) * DH] for h in chunk], axis=0)


def chunks_of(heads, size):
    return [range(start, start + size) for start in range(0, heads, size)]


def probs_kernel(seq_count, size, *refs):
    spots_ref, query_ref, grad_ref = refs[:3]
    part_refs = refs[3 : 3 + seq_count]
    probs_ref, rows_ref, keep_ref, ship_ref, library, total, sems = refs[3 + seq_count :]
    blocks_here = part_refs[0].shape[0]
    all_blocks = seq_count * blocks_here
    step = pl.program_id(0)
    begin(step, part_refs, library, total, sems)
    block = lax.axis_index("seq") * blocks_here + step
    spots = listed_spots(spots_ref, step)
    for number, spot in enumerate(spots):
        rows_ref[0, pl.ds(number * BLOCK, BLOCK), :] = library[spot]
    first_bias = jnp.where(block == 0, NEG_FILL, 0.0)
    last_bias = jnp.where(block == all_blocks - 1, NEG_FILL, 0.0)
    scale = DH ** (-0.5) * math.log2(math.e)
    terms = 0.0
    for chunk in chunks_of(query_ref.shape[1] // DH, size):
        query = stacked_heads(query_ref, chunk)
        grad = stacked_heads(grad_ref, chunk)
        scores = dot(rows_ref[0], query, 1, 1)
        scores = jnp.concatenate(
            [
                scores[:BLOCK] + first_bias,
                scores[BLOCK : 2 * BLOCK],
                scores[2 * BLOCK : 3 * BLOCK] + last_bias,
                scores[3 * BLOCK :],
            ],
            axis=0,
        )
        peak = jnp.max(scores, axis=0, keepdims=True)
        weights = jnp.exp2((scores - peak) * scale)
        probs = weights * (1.0 / jnp.sum(weights, axis=0, keepdims=True))
        probs16 = probs.astype(jnp.bfloat16)
        probs_ref[0, :, chunk[0] * BLOCK : (chunk[-1] + 1) * BLOCK] = probs16
        terms = terms + dot(probs16, grad, 1, 0)
    add_terms(total, spots, terms)
    finish(step, total, keep_ref, ship_ref)


def dscores_kernel(size, *refs):
    spots_ref, query_ref, grad_ref, probs_ref = refs[:4]
    part_refs, refs = refs[4:-8], refs[-8:]
    out_ref, dscores_ref, keep_ref, ship_ref, library, total, rows_ref, sems = refs
    step = pl.program_id(0)
    begin(step, part_refs, library, total, sems)
    spots = listed_spots(spots_ref, step)
    for number, spot in enumerate(spots):
        rows_ref[pl.ds(number * BLOCK, BLOCK), :] = library[spot]
    terms = 0.0
    for chunk in chunks_of(query_ref.shape[1] // DH, size):
        columns = slice(chunk[0] * BLOCK, (chunk[-1] + 1) * BLOCK)
        query = stacked_heads(query_ref, chunk)
        grad = stacked_heads(grad_ref, chunk)
        probs16 = probs_ref[0, :, columns]
        result = dot(rows_ref[...], probs16, 0, 0).astype(jnp.bfloat16).astype(jnp.float32)
        grad_across = jnp.transpose(grad.astype(jnp.float32))
        delta = jnp.sum(grad_across * result, axis=0, keepdims=True)
        dprobs = dot(rows_ref[...], grad, 1, 1)
        dscores = (probs16.astype(jnp.float32) * (dprobs - delta)).astype(jnp.bfloat16)
        dscores_ref[0, :, columns] = dscores
        terms = terms + dot(dscores, query, 1, 0)
        down = jnp.transpose(result).astype(jnp.bfloat16)
        for number, h in enumerate(chunk):
            out_ref[:, h * DH : (h + 1) * DH] = down[number * BLOCK : (number + 1) * BLOCK]
    add_terms(total, spots, terms * DH ** (-0.5))
    finish(step, total, keep_ref, ship_ref)


def dquery_kernel(size, dscores_ref, rows_ref, dquery_ref):
    for chunk in chunks_of(dquery_ref.shape[1] // DH, size):
        columns = slice(chunk[0] * BLOCK, (chunk[-1] + 1) * BLOCK)
        across = dot(rows_ref[0], dscores_ref[0, :, columns], 0, 0) * DH ** (-0.5)
        down = jnp.transpose(across).astype(jnp.bfloat16)
        for number, h in enumerate(chunk):
            dquery_ref[:, h * DH : (h + 1) * DH] = down[number * BLOCK : (number + 1) * BLOCK]


def small_grant():
    return pltpu.CompilerParams(vmem_limit_bytes=8 * 1024 * 1024)


def kernel_options(products, pairs):
    return {
        "compiler_params": pltpu.CompilerParams(vmem_limit_bytes=40 * 1024 * 1024),
        "cost_estimate": pl.CostEstimate(
            flops=4 * products * pairs * DH, bytes_accessed=4 * pairs, transcendentals=pairs
        ),
    }


def whole_body(queries, keys, values, d_out, rand_blocks, glob_blocks):
    seq_count = lax.axis_size("seq")
    head_count = lax.axis_size("head")
    short = keys.shape[0]
    tok_count, width = queries.shape
    heads_here = width // DH
    blocks_here = tok_count // BLOCK
    pair_count = seq_count // 2
    listed = (3 + GLOB + RAND) * BLOCK
    columns = heads_here * BLOCK
    pairs = blocks_here * listed * columns
    size = heads_here

    smem = pl.BlockSpec(memory_space=pltpu.SMEM)
    anywhere = pl.BlockSpec(memory_space=pl.ANY)
    tile_shape = jax.ShapeDtypeStruct(queries.shape, jnp.bfloat16)
    piece = jax.ShapeDtypeStruct((2 * short, DH), jnp.bfloat16)
    spots_shape = jax.ShapeDtypeStruct((blocks_here, 3 + GLOB + RAND), jnp.int32)
    rand_blocks, glob_blocks, keys, values, queries, d_out = [
        pltpu.with_memory_space_constraint(x, pltpu.HBM)
        for x in (rand_blocks, glob_blocks, keys, values, queries, d_out)
    ]
    pieces = pl.pallas_call(
        pack_kernel,
        in_specs=[anywhere] * 2,
        out_specs=[anywhere] * head_count,
        out_shape=[piece] * head_count,
        scratch_shapes=[pltpu.SemaphoreType.DMA((2 * head_count,))],
        compiler_params=small_grant(),
    )(keys, values)
    spots, query_here, grad_here = pl.pallas_call(
        lambda *refs: list_kernel(seq_count, *refs),
        in_specs=[anywhere] * 4,
        out_specs=[smem] + [anywhere] * 2,
        out_shape=[spots_shape, tile_shape, tile_shape],
        scratch_shapes=[
            pltpu.SMEM(rand_blocks.shape, jnp.int32),
            pltpu.SMEM(glob_blocks.shape, jnp.int32),
            pltpu.SemaphoreType.DMA((4,)),
        ],
        compiler_params=small_grant(),
        cost_estimate=pl.CostEstimate(
            flops=0, bytes_accessed=8 * tok_count * width, transcendentals=0
        ),
    )(rand_blocks, glob_blocks, queries, d_out)
    pieces = [pieces[0]] + [
        lax.ppermute(pieces[k], "head", flips(head_count, k)) for k in range(1, head_count)
    ]

    def along_far(own):
        parts = [own]
        for k in range(2, seq_count, 2):
            parts.append(lax.ppermute(own, "seq", flips(seq_count, k)))
        return parts

    def to_near(part):
        return lax.ppermute(part, "seq", flips(seq_count, 1))

    key_far = along_far(jnp.stack([p[:short] for p in pieces]))
    key_parts = [part for far in key_far for part in (far, to_near(far))]
    value_own = jnp.stack([p[short:] for p in pieces])
    value_pair = jnp.concatenate([value_own, to_near(value_own)])
    value_pair, _ = lax.optimization_barrier((value_pair, key_far[1:]))
    value_parts = along_far(value_pair)

    tile = pl.BlockSpec((BLOCK, width), lambda i: (i, 0))
    square = pl.BlockSpec((1, listed, columns), lambda i: (i, 0, 0))
    listing = pl.BlockSpec((1, listed, DH), lambda i: (i, 0, 0))
    half = (pair_count, blocks_here, BLOCK, DH)
    whole = pl.BlockSpec(half, lambda i: (0, 0, 0, 0))
    square_shape = jax.ShapeDtypeStruct((blocks_here, listed, columns), jnp.bfloat16)
    listing_shape = jax.ShapeDtypeStruct((blocks_here, listed, DH), jnp.bfloat16)
    keep_shape = jax.ShapeDtypeStruct(half, jnp.float32)
    ship_shape = jax.ShapeDtypeStruct(half, jnp.bfloat16)
    library = pltpu.VMEM((seq_count * blocks_here, BLOCK, DH), jnp.bfloat16)
    total = pltpu.VMEM((seq_count * blocks_here, BLOCK, DH), jnp.float32)
    sems = pltpu.SemaphoreType.DMA((seq_count,))

    probs, key_lists, value_keep, value_ship = pl.pallas_call(
        lambda *refs: probs_kernel(seq_count, size, *refs),
        grid=(blocks_here,),
        in_specs=[smem, tile, tile] + [anywhere] * len(key_parts),
        out_specs=[square, listing, whole, whole],
        out_shape=[square_shape, listing_shape, keep_shape, ship_shape],
        scratch_shapes=[library, total, sems],
        **kernel_options(2, pairs),
    )(spots, query_here, grad_here, *key_parts)
    value_near = lax.ppermute(value_ship, "seq", flips(seq_count, 1))
    attn_out, dscores, key_keep, key_ship = pl.pallas_call(
        lambda *refs: dscores_kernel(size, *refs),
        grid=(blocks_here,),
        in_specs=[smem, tile, tile, square] + [anywhere] * len(value_parts),
        out_specs=[tile, square, whole, whole],
        out_shape=[tile_shape, square_shape, keep_shape, ship_shape],
        scratch_shapes=[library, total, pltpu.VMEM((listed, DH), jnp.bfloat16), sems],
        **kernel_options(3, pairs),
    )(spots, query_here, grad_here, probs, *value_parts)
    key_near = lax.ppermute(key_ship, "seq", flips(seq_count, 1))

    def sums_of(keep, near):
        sums = keep + near.astype(jnp.float32)
        return sums[0], [sums[pair].astype(jnp.bfloat16) for pair in range(1, pair_count)]

    def from_far(sums):
        return [
            lax.ppermute(sums[pair - 1], "seq", flips(seq_count, 2 * pair))
            for pair in range(1, pair_count)
        ]

    def added(own, far):
        for part in far:
            own = own + part.astype(jnp.float32)
        return own

    key_own, key_sums = sums_of(key_keep, key_near)
    key_far = from_far(key_sums)
    value_own, value_sums = sums_of(value_keep, value_near)
    value_far = from_far(value_sums)
    d_queries = pl.pallas_call(
        lambda *refs: dquery_kernel(size, *refs),
        grid=(blocks_here,),
        in_specs=[square, listing],
        out_specs=tile,
        out_shape=tile_shape,
        **kernel_options(1, pairs),
    )(*lax.optimization_barrier((dscores, key_lists, key_sums))[:2])

    key_far, value_far, d_queries = lax.optimization_barrier((key_far, value_far, d_queries))
    packed = jnp.concatenate(
        [added(key_own, key_far), added(value_own, value_far)], axis=1
    ).astype(jnp.bfloat16)
    back = [packed[0]] + [
        lax.ppermute(packed[k], "head", flips(head_count, k)) for k in range(1, head_count)
    ]
    flat = jax.ShapeDtypeStruct(keys.shape, jnp.bfloat16)
    d_keys, d_values = pl.pallas_call(
        unpack_kernel, out_shape=[flat, flat], compiler_params=small_grant()
    )(*back)
    return (attn_out, d_queries, d_keys, d_values)


def body(queries, keys, values, d_out, rand_blocks, glob_blocks):
    seq_count = lax.axis_size("seq")
    head_count = lax.axis_size("head")
    blocks_here = rand_blocks.shape[0]
    capacity = -(-rand_blocks.size // seq_count)
    powers = all(n & (n - 1) == 0 for n in (seq_count, head_count))
    fits = keys.shape[0] == BLOCK and blocks_here == head_count
    if capacity >= blocks_here and seq_count > 1 and powers and fits:
        return whole_body(queries, keys, values, d_out, rand_blocks, glob_blocks)
    return request_body(queries, keys, values, d_out, rand_blocks, glob_blocks)


def solution(mesh):
    in_specs = (
        P("seq", "head"),
        P(("seq", "head"), None),
        P(("seq", "head"), None),
        P("seq", "head"),
        P("seq", None),
        P(),
    )
    out_specs = (
        P("seq", "head"),
        P("seq", "head"),
        P(("seq", "head"), None),
        P(("seq", "head"), None),
    )
    return jax.shard_map(body, mesh=mesh, in_specs=in_specs, out_specs=out_specs, check_vma=False)
```

```python
import math

import jax
import jax.numpy as jnp
from jax import lax
from jax.experimental import pallas as pl
from jax.experimental.pallas import tpu as pltpu
from jax.sharding import PartitionSpec as P

DH = 128
KVH = 4
BLOCK = 64
GLOB = 2
RAND = 8


NEG_FILL = -1e30


def padded_2(cells, sides, width):
    for axis, dim in sides:
        count = lax.axis_size(axis)
        ends = count - 1
        head = lax.slice_in_dim(cells, 0, width, axis=dim)
        tail = lax.slice_in_dim(cells, cells.shape[dim] - width, cells.shape[dim], axis=dim)
        cells = jnp.concatenate(
            [
                lax.ppermute(tail, axis, [(i, (i + 1) % count) for i in range(ends)]),
                cells,
                lax.ppermute(head, axis, [((i + 1) % count, i) for i in range(ends)]),
            ],
            axis=dim,
        )
    return cells


def broadcast(block, axis, source):
    block = jnp.where(lax.axis_index(axis) == source, block, jnp.zeros_like(block))
    return lax.psum(block, axis)


def key_rows(library, spots):
    chosen = jnp.stack(
        [
            lax.dynamic_index_in_dim(library, spots[i], 0, keepdims=False)
            for i in range(spots.shape[0])
        ]
    )
    flat = chosen.reshape(chosen.shape[0] * chosen.shape[1], chosen.shape[2])
    return (flat[:, :DH], flat[:, DH:])


def masked_scores(query_block, keys_here, allowed_row):
    factor = DH ** (-0.5)
    scores = (
        jnp.einsum("thd,kd->htk", query_block, keys_here, preferred_element_type=jnp.float32)
        * factor
    )
    widened = jnp.repeat(allowed_row, keys_here.shape[0] // allowed_row.shape[0])
    return jnp.where(widened[None, None, :], scores, NEG_FILL)


def request_body(queries, keys, values, d_out, rand_blocks, glob_blocks):
    seq_count = lax.axis_size("seq")
    here = lax.axis_index("seq")
    short = keys.shape[0]
    stacked = jnp.concatenate(
        [keys.reshape(short, KVH, DH), values.reshape(short, KVH, DH)], axis=2
    )
    mine = lax.all_to_all(stacked, "head", split_axis=1, concat_axis=0, tiled=True)
    tok_count = mine.shape[0]
    blocks_here = tok_count // BLOCK
    flat_pairs = mine.reshape(tok_count, 2 * DH)
    own_blocks = flat_pairs.reshape(blocks_here, BLOCK, 2 * DH)
    padded = padded_2(flat_pairs, (("seq", 0),), BLOCK)
    window = padded.reshape(blocks_here + 2, BLOCK, 2 * DH)
    global_parts = []
    for number in range(GLOB):
        target = glob_blocks[number]
        piece = lax.dynamic_index_in_dim(own_blocks, target % blocks_here, 0, keepdims=False)
        global_parts.append(broadcast(piece, "seq", target // blocks_here))
    global_pairs = jnp.stack(global_parts)
    entries = rand_blocks.reshape(-1)
    entry_count = entries.shape[0]
    capacity = -(-entry_count // seq_count)
    position_count = seq_count * capacity
    owners = entries // blocks_here
    inner_index = entries % blocks_here
    order = jnp.arange(entry_count, dtype=jnp.int32)
    earlier = (owners[:, None] == owners[None, :]) & (order[:, None] > order[None, :])
    ranks = jnp.sum(earlier.astype(jnp.int32), axis=1)
    slots = owners * capacity + ranks
    placing = slots[None, :] == jnp.arange(position_count, dtype=jnp.int32)[:, None]
    wanted = jnp.sum(jnp.where(placing, inner_index[None, :], 0), axis=1).reshape(
        seq_count, capacity
    )
    incoming = lax.all_to_all(wanted, "seq", split_axis=0, concat_axis=0, tiled=True).reshape(
        position_count
    )
    block_ids = jnp.arange(blocks_here, dtype=jnp.int32)
    picking = (incoming[:, None] == block_ids[None, :]).astype(jnp.bfloat16)
    served = (
        jnp.dot(
            picking,
            own_blocks.reshape(blocks_here, BLOCK * 2 * DH),
            preferred_element_type=jnp.float32,
        )
        .astype(jnp.bfloat16)
        .reshape(seq_count, capacity, BLOCK, 2 * DH)
    )
    fetched = lax.all_to_all(served, "seq", split_axis=0, concat_axis=0, tiled=True).reshape(
        position_count, BLOCK, 2 * DH
    )
    window_ids = jnp.stack([block_ids, block_ids + 1, block_ids + 2], axis=1)
    global_ids = jnp.broadcast_to(
        blocks_here + 2 + jnp.arange(GLOB, dtype=jnp.int32), (blocks_here, GLOB)
    )
    random_ids = blocks_here + 2 + GLOB + slots.reshape(blocks_here, RAND)
    positions = jnp.concatenate([window_ids, global_ids, random_ids], axis=1)
    allowed = jnp.concatenate(
        [
            jnp.logical_not((block_ids == 0) & (here == 0))[:, None],
            jnp.ones((blocks_here, 1), jnp.bool_),
            jnp.logical_not((block_ids == blocks_here - 1) & (here == seq_count - 1))[:, None],
            jnp.ones((blocks_here, GLOB + RAND), jnp.bool_),
        ],
        axis=1,
    )
    library = jnp.concatenate([window, global_pairs, fetched], axis=0)
    heads_here = queries.shape[1] // DH
    query_blocks = queries.reshape(blocks_here, BLOCK, heads_here, DH)
    grad_blocks = d_out.reshape(blocks_here, BLOCK, heads_here, DH)

    def forward_step(inputs):
        query_block, spots, allowed_row = inputs
        keys_here, values_here = key_rows(library, spots)
        scores = masked_scores(query_block, keys_here, allowed_row)
        peak = jnp.max(scores, axis=-1, keepdims=True)
        logsum = peak + jnp.log(jnp.sum(jnp.exp(scores - peak), axis=-1, keepdims=True))
        probs16 = jnp.exp(scores - logsum).astype(jnp.bfloat16)
        result = jnp.einsum("htk,kd->thd", probs16, values_here, preferred_element_type=jnp.float32)
        return (result.astype(jnp.bfloat16), logsum)

    out_blocks, logsums = lax.map(forward_step, (query_blocks, positions, allowed))
    refetched = lax.all_to_all(served, "seq", split_axis=0, concat_axis=0, tiled=True).reshape(
        position_count, BLOCK, 2 * DH
    )
    library_back = jnp.concatenate([window, global_pairs, refetched], axis=0)

    def backward_step(inputs):
        query_block, gradient_tile, out_block, logsum, spots, allowed_row = inputs
        keys_here, values_here = key_rows(library_back, spots)
        factor = DH ** (-0.5)
        scores = masked_scores(query_block, keys_here, allowed_row)
        probs = jnp.exp(scores - logsum)
        probs16 = probs.astype(jnp.bfloat16)
        delta = jnp.sum(gradient_tile.astype(jnp.float32) * out_block.astype(jnp.float32), axis=-1)
        dprobs = jnp.einsum(
            "thd,kd->htk", gradient_tile, values_here, preferred_element_type=jnp.float32
        )
        dscores = (probs * (dprobs - jnp.transpose(delta)[:, :, None])).astype(jnp.bfloat16)
        dquery = (
            jnp.einsum("htk,kd->thd", dscores, keys_here, preferred_element_type=jnp.float32)
            * factor
        )
        dkey = (
            jnp.einsum("htk,thd->kd", dscores, query_block, preferred_element_type=jnp.float32)
            * factor
        )
        dvalue = jnp.einsum(
            "htk,thd->kd", probs16, gradient_tile, preferred_element_type=jnp.float32
        )
        terms = jnp.concatenate([dkey, dvalue], axis=1).reshape(spots.shape[0], BLOCK, 2 * DH)
        return (dquery.astype(jnp.bfloat16), terms)

    dquery_blocks, terms = lax.map(
        backward_step, (query_blocks, grad_blocks, out_blocks, logsums, positions, allowed)
    )
    attn_out = out_blocks.reshape(tok_count, heads_here * DH)
    d_queries = dquery_blocks.reshape(tok_count, heads_here * DH)
    prev_terms = terms[:, 0]
    self_terms = terms[:, 1]
    next_terms = terms[:, 2]
    zero_block = jnp.zeros((1, BLOCK, 2 * DH), jnp.float32)
    grads = (
        self_terms
        + jnp.concatenate([prev_terms[1:], zero_block], axis=0)
        + jnp.concatenate([zero_block, next_terms[:-1]], axis=0)
    )
    rims = jnp.concatenate([prev_terms[0], next_terms[-1]], axis=0).astype(jnp.bfloat16)
    arrived = padded_2(rims, (("seq", 0),), BLOCK)
    from_left = arrived[:BLOCK].astype(jnp.float32)
    from_right = arrived[3 * BLOCK :].astype(jnp.float32)
    edge_first = jnp.concatenate(
        [from_left[None], jnp.zeros((blocks_here - 1, BLOCK, 2 * DH), jnp.float32)], axis=0
    )
    edge_last = jnp.concatenate(
        [jnp.zeros((blocks_here - 1, BLOCK, 2 * DH), jnp.float32), from_right[None]], axis=0
    )
    grads = grads + edge_first + edge_last
    global_terms = jnp.sum(terms[:, 3 : 3 + GLOB], axis=0)
    global_total = lax.psum(global_terms, "seq")
    global_hits = ((glob_blocks // blocks_here)[:, None] == here) & (
        (glob_blocks % blocks_here)[:, None] == block_ids[None, :]
    )
    grads = grads + jnp.sum(
        jnp.where(global_hits[:, :, None, None], global_total[:, None], 0.0), axis=0
    )
    random_terms = terms[:, 3 + GLOB :].reshape(entry_count, BLOCK * 2 * DH).astype(jnp.bfloat16)
    outgoing = jnp.dot(
        placing.astype(jnp.bfloat16), random_terms, preferred_element_type=jnp.float32
    ).astype(jnp.bfloat16)
    returned = lax.all_to_all(
        outgoing.reshape(seq_count, capacity, BLOCK, 2 * DH),
        "seq",
        split_axis=0,
        concat_axis=0,
        tiled=True,
    )
    landing = (incoming[None, :] == block_ids[:, None]).astype(jnp.bfloat16)
    grads = grads + jnp.dot(
        landing,
        returned.reshape(position_count, BLOCK * 2 * DH),
        preferred_element_type=jnp.float32,
    ).reshape(blocks_here, BLOCK, 2 * DH)
    packed = grads.astype(jnp.bfloat16).reshape(tok_count, 1, 2 * DH)
    restored = lax.all_to_all(packed, "head", split_axis=0, concat_axis=1, tiled=True)
    d_keys = restored[:, :, :DH].reshape(short, KVH * DH)
    d_values = restored[:, :, DH:].reshape(short, KVH * DH)
    return (attn_out, d_queries, d_keys, d_values)


def flips(count, bits):
    return [(i, i ^ bits) for i in range(count)]


def head_columns(head, offset):
    return pl.ds(pl.multiple_of((head ^ offset) * DH, DH), DH)


def run_copies(copies):
    for copy in copies:
        copy.start()
    for copy in copies:
        copy.wait()


def pack_kernel(*refs):
    keys_ref, values_ref, *piece_refs, sems = refs
    head = lax.axis_index("head")
    short = keys_ref.shape[0]
    moves = []
    for offset, piece in enumerate(piece_refs):
        columns = head_columns(head, offset)
        moves.append((keys_ref.at[:, columns], piece.at[pl.ds(0, short)]))
        moves.append((values_ref.at[:, columns], piece.at[pl.ds(short, short)]))
    run_copies([pltpu.make_async_copy(a, b, sems.at[n]) for n, (a, b) in enumerate(moves)])


def list_kernel(seq_count, *refs):
    rand_from, glob_from, query_from, grad_from = refs[:4]
    spots_ref, query_ref, grad_ref, rand_ref, glob_ref, sems = refs[4:]
    here = lax.axis_index("seq")
    head = lax.axis_index("head")
    moves = [(rand_from, rand_ref), (glob_from, glob_ref)]
    moves += [(query_from, query_ref), (grad_from, grad_ref)]
    copies = [pltpu.make_async_copy(a, b, sems.at[n]) for n, (a, b) in enumerate(moves)]
    for copy in copies:
        copy.start()
    copies[0].wait()
    copies[1].wait()
    blocks_here = rand_ref.shape[0]
    last = seq_count * blocks_here - 1
    for step in range(blocks_here):
        block = here * blocks_here + step
        names = [jnp.maximum(block - 1, 0), block, jnp.minimum(block + 1, last)]
        names += [glob_ref[i] for i in range(GLOB)]
        names += [rand_ref[step, i] for i in range(RAND)]
        for number, name in enumerate(names):
            owner = lax.div(name, blocks_here) ^ here
            spots_ref[step, number] = owner * blocks_here + (lax.rem(name, blocks_here) ^ head)
    copies[2].wait()
    copies[3].wait()


def unpack_kernel(*refs):
    piece_refs, (keys_ref, values_ref) = refs[:-2], refs[-2:]
    head = lax.axis_index("head")
    short = keys_ref.shape[0]
    for offset, piece in enumerate(piece_refs):
        columns = head_columns(head, offset)
        keys_ref[:, columns] = piece[:short, :]
        values_ref[:, columns] = piece[short:, :]


def dot(left, right, left_dim, right_dim):
    return lax.dot_general(
        left,
        right,
        (((left_dim,), (right_dim,)), ((), ())),
        preferred_element_type=jnp.float32,
    )


def listed_spots(spots_ref, step):
    return [spots_ref[step, number] for number in range(spots_ref.shape[1])]


def begin(part_refs, library, total):
    at = 0
    for part in part_refs:
        library[at : at + part.shape[0]] = part[...]
        at += part.shape[0]
    total[...] = jnp.zeros_like(total)


def add_terms(total, spots, terms):
    for number, spot in enumerate(spots):
        total[spot] += terms[number * BLOCK : (number + 1) * BLOCK]


def finish(total, keep_ref, ship_ref):
    pairs, size = keep_ref.shape[:2]
    for pair in range(pairs):
        keep_ref[pair] = total[pl.ds(2 * pair * size, size)]
        ship_ref[pair] = total[pl.ds((2 * pair + 1) * size, size)].astype(jnp.bfloat16)


def stacked_heads(ref, step, chunk):
    rows = slice(step * BLOCK, (step + 1) * BLOCK)
    return jnp.concatenate([ref[rows, h * DH : (h + 1) * DH] for h in chunk], axis=0)


def chunks_of(heads, size):
    return [range(start, start + size) for start in range(0, heads, size)]


def probs_kernel(seq_count, size, *refs):
    spots_ref, query_ref, grad_ref = refs[:3]
    part_refs = refs[3 : 3 + seq_count]
    probs_ref, rows_ref, keep_ref, ship_ref, library, total = refs[3 + seq_count :]
    blocks_here = probs_ref.shape[0]
    all_blocks = library.shape[0]
    begin(part_refs, library, total)
    for step in range(blocks_here):
        block = lax.axis_index("seq") * blocks_here + step
        spots = listed_spots(spots_ref, step)
        for number, spot in enumerate(spots):
            rows_ref[step, pl.ds(number * BLOCK, BLOCK), :] = library[spot]
        first_bias = jnp.where(block == 0, NEG_FILL, 0.0)
        last_bias = jnp.where(block == all_blocks - 1, NEG_FILL, 0.0)
        scale = DH ** (-0.5) * math.log2(math.e)
        terms = 0.0
        for chunk in chunks_of(query_ref.shape[1] // DH, size):
            query = stacked_heads(query_ref, step, chunk)
            grad = stacked_heads(grad_ref, step, chunk)
            scores = dot(rows_ref[step], query, 1, 1)
            scores = jnp.concatenate(
                [
                    scores[:BLOCK] + first_bias,
                    scores[BLOCK : 2 * BLOCK],
                    scores[2 * BLOCK : 3 * BLOCK] + last_bias,
                    scores[3 * BLOCK :],
                ],
                axis=0,
            )
            peak = jnp.max(scores, axis=0, keepdims=True)
            weights = jnp.exp2((scores - peak) * scale)
            probs = weights * (1.0 / jnp.sum(weights, axis=0, keepdims=True))
            probs16 = probs.astype(jnp.bfloat16)
            probs_ref[step, :, chunk[0] * BLOCK : (chunk[-1] + 1) * BLOCK] = probs16
            terms = terms + dot(probs16, grad, 1, 0)
        add_terms(total, spots, terms)
    finish(total, keep_ref, ship_ref)


def send_tile(stage, out_ref, step, sems):
    rows = pl.ds(step * BLOCK, BLOCK)
    copy = pltpu.make_async_copy(stage.at[step], out_ref.at[rows], sems.at[step])
    copy.start()
    return copy


def dscores_kernel(size, *refs):
    spots_ref, query_ref, grad_ref, probs_ref = refs[:4]
    part_refs, refs = refs[4:-9], refs[-9:]
    out_ref, dscores_ref, keep_ref, ship_ref, library, total, rows_ref, stage, sems = refs
    begin(part_refs, library, total)
    copies = []
    for step in range(stage.shape[0]):
        spots = listed_spots(spots_ref, step)
        for number, spot in enumerate(spots):
            rows_ref[step, pl.ds(number * BLOCK, BLOCK), :] = library[spot]
        terms = 0.0
        for chunk in chunks_of(query_ref.shape[1] // DH, size):
            columns = slice(chunk[0] * BLOCK, (chunk[-1] + 1) * BLOCK)
            query = stacked_heads(query_ref, step, chunk)
            grad = stacked_heads(grad_ref, step, chunk)
            probs16 = probs_ref[step, :, columns]
            result = dot(rows_ref[step], probs16, 0, 0).astype(jnp.bfloat16).astype(jnp.float32)
            grad_across = jnp.transpose(grad.astype(jnp.float32))
            delta = jnp.sum(grad_across * result, axis=0, keepdims=True)
            dprobs = dot(rows_ref[step], grad, 1, 1)
            dscores = (probs16.astype(jnp.float32) * (dprobs - delta)).astype(jnp.bfloat16)
            dscores_ref[step, :, columns] = dscores
            terms = terms + dot(dscores, query, 1, 0)
            down = jnp.transpose(result).astype(jnp.bfloat16)
            for number, h in enumerate(chunk):
                stage[step, :, h * DH : (h + 1) * DH] = down[number * BLOCK : (number + 1) * BLOCK]
        add_terms(total, spots, terms * DH ** (-0.5))
        copies.append(send_tile(stage, out_ref, step, sems))
    finish(total, keep_ref, ship_ref)
    for copy in copies:
        copy.wait()


def dquery_kernel(size, dscores_ref, rows_ref, dquery_ref, stage, sems):
    copies = []
    for step in range(stage.shape[0]):
        for chunk in chunks_of(dquery_ref.shape[1] // DH, size):
            columns = slice(chunk[0] * BLOCK, (chunk[-1] + 1) * BLOCK)
            across = dot(rows_ref[step], dscores_ref[step, :, columns], 0, 0) * DH ** (-0.5)
            down = jnp.transpose(across).astype(jnp.bfloat16)
            for number, h in enumerate(chunk):
                rows = slice(number * BLOCK, (number + 1) * BLOCK)
                stage[step, :, h * DH : (h + 1) * DH] = down[rows]
        copies.append(send_tile(stage, dquery_ref, step, sems))
    for copy in copies:
        copy.wait()


def small_grant():
    return pltpu.CompilerParams(vmem_limit_bytes=8 * 1024 * 1024)


def kernel_options(products, pairs):
    return {
        "compiler_params": pltpu.CompilerParams(vmem_limit_bytes=36 * 1024 * 1024),
        "cost_estimate": pl.CostEstimate(
            flops=4 * products * pairs * DH, bytes_accessed=4 * pairs, transcendentals=pairs
        ),
    }


def whole_body(queries, keys, values, d_out, rand_blocks, glob_blocks):
    seq_count = lax.axis_size("seq")
    head_count = lax.axis_size("head")
    short = keys.shape[0]
    tok_count, width = queries.shape
    heads_here = width // DH
    blocks_here = tok_count // BLOCK
    pair_count = seq_count // 2
    listed = (3 + GLOB + RAND) * BLOCK
    columns = heads_here * BLOCK
    pairs = blocks_here * listed * columns
    size = heads_here

    smem = pl.BlockSpec(memory_space=pltpu.SMEM)
    anywhere = pl.BlockSpec(memory_space=pl.ANY)
    tile_shape = jax.ShapeDtypeStruct(queries.shape, jnp.bfloat16)
    piece = jax.ShapeDtypeStruct((2 * short, DH), jnp.bfloat16)
    spots_shape = jax.ShapeDtypeStruct((blocks_here, 3 + GLOB + RAND), jnp.int32)
    rand_blocks, glob_blocks, keys, values, queries, d_out = [
        pltpu.with_memory_space_constraint(x, pltpu.HBM)
        for x in (rand_blocks, glob_blocks, keys, values, queries, d_out)
    ]
    pieces = pl.pallas_call(
        pack_kernel,
        in_specs=[anywhere] * 2,
        out_specs=[anywhere] * head_count,
        out_shape=[piece] * head_count,
        scratch_shapes=[pltpu.SemaphoreType.DMA((2 * head_count,))],
        compiler_params=small_grant(),
    )(keys, values)
    spots, query_here, grad_here = pl.pallas_call(
        lambda *refs: list_kernel(seq_count, *refs),
        in_specs=[anywhere] * 4,
        out_specs=[smem] + [anywhere] * 2,
        out_shape=[spots_shape, tile_shape, tile_shape],
        scratch_shapes=[
            pltpu.SMEM(rand_blocks.shape, jnp.int32),
            pltpu.SMEM(glob_blocks.shape, jnp.int32),
            pltpu.SemaphoreType.DMA((4,)),
        ],
        compiler_params=small_grant(),
        cost_estimate=pl.CostEstimate(
            flops=0, bytes_accessed=8 * tok_count * width, transcendentals=0
        ),
    )(rand_blocks, glob_blocks, queries, d_out)
    pieces = [pieces[0]] + [
        lax.ppermute(pieces[k], "head", flips(head_count, k)) for k in range(1, head_count)
    ]

    def along_far(own):
        parts = [own]
        for k in range(2, seq_count, 2):
            parts.append(lax.ppermute(own, "seq", flips(seq_count, k)))
        return parts

    def to_near(part):
        return lax.ppermute(part, "seq", flips(seq_count, 1))

    key_far = along_far(jnp.stack([p[:short] for p in pieces]))
    key_parts = [part for far in key_far for part in (far, to_near(far))]
    value_own = jnp.stack([p[short:] for p in pieces])
    value_pair = jnp.concatenate([value_own, to_near(value_own)])
    value_pair, _ = lax.optimization_barrier((value_pair, key_far[1:]))
    value_parts = along_far(value_pair)

    lists = pltpu.VMEM((blocks_here, listed, DH), jnp.bfloat16)
    stage = pltpu.VMEM((blocks_here, BLOCK, width), jnp.bfloat16)
    tile_sems = pltpu.SemaphoreType.DMA((blocks_here,))
    vmem = pl.BlockSpec(memory_space=pltpu.VMEM)
    half = (pair_count, blocks_here, BLOCK, DH)
    square_shape = jax.ShapeDtypeStruct((blocks_here, listed, columns), jnp.bfloat16)
    listing_shape = jax.ShapeDtypeStruct((blocks_here, listed, DH), jnp.bfloat16)
    keep_shape = jax.ShapeDtypeStruct(half, jnp.float32)
    ship_shape = jax.ShapeDtypeStruct(half, jnp.bfloat16)
    library = pltpu.VMEM((seq_count * blocks_here, BLOCK, DH), jnp.bfloat16)
    total = pltpu.VMEM((seq_count * blocks_here, BLOCK, DH), jnp.float32)

    probs, key_lists, value_keep, value_ship = pl.pallas_call(
        lambda *refs: probs_kernel(seq_count, size, *refs),
        in_specs=[smem, vmem, vmem] + [vmem] * len(key_parts),
        out_specs=[vmem] * 4,
        out_shape=[square_shape, listing_shape, keep_shape, ship_shape],
        scratch_shapes=[library, total],
        **kernel_options(2, pairs),
    )(spots, query_here, grad_here, *key_parts)
    value_near = lax.ppermute(value_ship, "seq", flips(seq_count, 1))
    attn_out, dscores, key_keep, key_ship = pl.pallas_call(
        lambda *refs: dscores_kernel(size, *refs),
        in_specs=[smem, vmem, vmem, vmem] + [vmem] * len(value_parts),
        out_specs=[anywhere, vmem, vmem, vmem],
        out_shape=[tile_shape, square_shape, keep_shape, ship_shape],
        scratch_shapes=[library, total, lists, stage, tile_sems],
        **kernel_options(3, pairs),
    )(spots, query_here, grad_here, probs, *value_parts)
    key_near = lax.ppermute(key_ship, "seq", flips(seq_count, 1))

    def sums_of(keep, near):
        sums = keep + near.astype(jnp.float32)
        return sums[0], [sums[pair].astype(jnp.bfloat16) for pair in range(1, pair_count)]

    def from_far(sums):
        return [
            lax.ppermute(sums[pair - 1], "seq", flips(seq_count, 2 * pair))
            for pair in range(1, pair_count)
        ]

    def added(own, far):
        for part in far:
            own = own + part.astype(jnp.float32)
        return own

    key_own, key_sums = sums_of(key_keep, key_near)
    key_far = from_far(key_sums)
    value_own, value_sums = sums_of(value_keep, value_near)
    value_far = from_far(value_sums)
    d_queries = pl.pallas_call(
        lambda *refs: dquery_kernel(size, *refs),
        in_specs=[vmem, vmem],
        out_specs=anywhere,
        out_shape=tile_shape,
        scratch_shapes=[stage, tile_sems],
        **kernel_options(1, pairs),
    )(*lax.optimization_barrier((dscores, key_lists, key_sums))[:2])

    key_far, value_far, d_queries = lax.optimization_barrier((key_far, value_far, d_queries))
    packed = jnp.concatenate(
        [added(key_own, key_far), added(value_own, value_far)], axis=1
    ).astype(jnp.bfloat16)
    back = [packed[0]] + [
        lax.ppermute(packed[k], "head", flips(head_count, k)) for k in range(1, head_count)
    ]
    flat = jax.ShapeDtypeStruct(keys.shape, jnp.bfloat16)
    d_keys, d_values = pl.pallas_call(
        unpack_kernel, out_shape=[flat, flat], compiler_params=small_grant()
    )(*back)
    return (attn_out, d_queries, d_keys, d_values)


def body(queries, keys, values, d_out, rand_blocks, glob_blocks):
    seq_count = lax.axis_size("seq")
    head_count = lax.axis_size("head")
    blocks_here = rand_blocks.shape[0]
    capacity = -(-rand_blocks.size // seq_count)
    powers = all(n & (n - 1) == 0 for n in (seq_count, head_count))
    fits = keys.shape[0] == BLOCK and blocks_here == head_count
    if capacity >= blocks_here and seq_count > 1 and powers and fits:
        return whole_body(queries, keys, values, d_out, rand_blocks, glob_blocks)
    return request_body(queries, keys, values, d_out, rand_blocks, glob_blocks)


def solution(mesh):
    in_specs = (
        P("seq", "head"),
        P(("seq", "head"), None),
        P(("seq", "head"), None),
        P("seq", "head"),
        P("seq", None),
        P(),
    )
    out_specs = (
        P("seq", "head"),
        P("seq", "head"),
        P(("seq", "head"), None),
        P(("seq", "head"), None),
    )
    return jax.shard_map(body, mesh=mesh, in_specs=in_specs, out_specs=out_specs, check_vma=False)
```

```python
import math

import jax
import jax.numpy as jnp
from jax import lax
from jax.experimental import pallas as pl
from jax.experimental.pallas import tpu as pltpu
from jax.sharding import PartitionSpec as P

DH = 128
KVH = 4
BLOCK = 64
GLOB = 2
RAND = 8


NEG_FILL = -1e30


def padded_2(cells, sides, width):
    for axis, dim in sides:
        count = lax.axis_size(axis)
        ends = count - 1
        head = lax.slice_in_dim(cells, 0, width, axis=dim)
        tail = lax.slice_in_dim(cells, cells.shape[dim] - width, cells.shape[dim], axis=dim)
        cells = jnp.concatenate(
            [
                lax.ppermute(tail, axis, [(i, (i + 1) % count) for i in range(ends)]),
                cells,
                lax.ppermute(head, axis, [((i + 1) % count, i) for i in range(ends)]),
            ],
            axis=dim,
        )
    return cells


def broadcast(block, axis, source):
    block = jnp.where(lax.axis_index(axis) == source, block, jnp.zeros_like(block))
    return lax.psum(block, axis)


def key_rows(library, spots):
    chosen = jnp.stack(
        [
            lax.dynamic_index_in_dim(library, spots[i], 0, keepdims=False)
            for i in range(spots.shape[0])
        ]
    )
    flat = chosen.reshape(chosen.shape[0] * chosen.shape[1], chosen.shape[2])
    return (flat[:, :DH], flat[:, DH:])


def masked_scores(query_block, keys_here, allowed_row):
    factor = DH ** (-0.5)
    scores = (
        jnp.einsum("thd,kd->htk", query_block, keys_here, preferred_element_type=jnp.float32)
        * factor
    )
    widened = jnp.repeat(allowed_row, keys_here.shape[0] // allowed_row.shape[0])
    return jnp.where(widened[None, None, :], scores, NEG_FILL)


def request_body(queries, keys, values, d_out, rand_blocks, glob_blocks):
    seq_count = lax.axis_size("seq")
    here = lax.axis_index("seq")
    short = keys.shape[0]
    stacked = jnp.concatenate(
        [keys.reshape(short, KVH, DH), values.reshape(short, KVH, DH)], axis=2
    )
    mine = lax.all_to_all(stacked, "head", split_axis=1, concat_axis=0, tiled=True)
    tok_count = mine.shape[0]
    blocks_here = tok_count // BLOCK
    flat_pairs = mine.reshape(tok_count, 2 * DH)
    own_blocks = flat_pairs.reshape(blocks_here, BLOCK, 2 * DH)
    padded = padded_2(flat_pairs, (("seq", 0),), BLOCK)
    window = padded.reshape(blocks_here + 2, BLOCK, 2 * DH)
    global_parts = []
    for number in range(GLOB):
        target = glob_blocks[number]
        piece = lax.dynamic_index_in_dim(own_blocks, target % blocks_here, 0, keepdims=False)
        global_parts.append(broadcast(piece, "seq", target // blocks_here))
    global_pairs = jnp.stack(global_parts)
    entries = rand_blocks.reshape(-1)
    entry_count = entries.shape[0]
    capacity = -(-entry_count // seq_count)
    position_count = seq_count * capacity
    owners = entries // blocks_here
    inner_index = entries % blocks_here
    order = jnp.arange(entry_count, dtype=jnp.int32)
    earlier = (owners[:, None] == owners[None, :]) & (order[:, None] > order[None, :])
    ranks = jnp.sum(earlier.astype(jnp.int32), axis=1)
    slots = owners * capacity + ranks
    placing = slots[None, :] == jnp.arange(position_count, dtype=jnp.int32)[:, None]
    wanted = jnp.sum(jnp.where(placing, inner_index[None, :], 0), axis=1).reshape(
        seq_count, capacity
    )
    incoming = lax.all_to_all(wanted, "seq", split_axis=0, concat_axis=0, tiled=True).reshape(
        position_count
    )
    block_ids = jnp.arange(blocks_here, dtype=jnp.int32)
    picking = (incoming[:, None] == block_ids[None, :]).astype(jnp.bfloat16)
    served = (
        jnp.dot(
            picking,
            own_blocks.reshape(blocks_here, BLOCK * 2 * DH),
            preferred_element_type=jnp.float32,
        )
        .astype(jnp.bfloat16)
        .reshape(seq_count, capacity, BLOCK, 2 * DH)
    )
    fetched = lax.all_to_all(served, "seq", split_axis=0, concat_axis=0, tiled=True).reshape(
        position_count, BLOCK, 2 * DH
    )
    window_ids = jnp.stack([block_ids, block_ids + 1, block_ids + 2], axis=1)
    global_ids = jnp.broadcast_to(
        blocks_here + 2 + jnp.arange(GLOB, dtype=jnp.int32), (blocks_here, GLOB)
    )
    random_ids = blocks_here + 2 + GLOB + slots.reshape(blocks_here, RAND)
    positions = jnp.concatenate([window_ids, global_ids, random_ids], axis=1)
    allowed = jnp.concatenate(
        [
            jnp.logical_not((block_ids == 0) & (here == 0))[:, None],
            jnp.ones((blocks_here, 1), jnp.bool_),
            jnp.logical_not((block_ids == blocks_here - 1) & (here == seq_count - 1))[:, None],
            jnp.ones((blocks_here, GLOB + RAND), jnp.bool_),
        ],
        axis=1,
    )
    library = jnp.concatenate([window, global_pairs, fetched], axis=0)
    heads_here = queries.shape[1] // DH
    query_blocks = queries.reshape(blocks_here, BLOCK, heads_here, DH)
    grad_blocks = d_out.reshape(blocks_here, BLOCK, heads_here, DH)

    def forward_step(inputs):
        query_block, spots, allowed_row = inputs
        keys_here, values_here = key_rows(library, spots)
        scores = masked_scores(query_block, keys_here, allowed_row)
        peak = jnp.max(scores, axis=-1, keepdims=True)
        logsum = peak + jnp.log(jnp.sum(jnp.exp(scores - peak), axis=-1, keepdims=True))
        probs16 = jnp.exp(scores - logsum).astype(jnp.bfloat16)
        result = jnp.einsum("htk,kd->thd", probs16, values_here, preferred_element_type=jnp.float32)
        return (result.astype(jnp.bfloat16), logsum)

    out_blocks, logsums = lax.map(forward_step, (query_blocks, positions, allowed))
    refetched = lax.all_to_all(served, "seq", split_axis=0, concat_axis=0, tiled=True).reshape(
        position_count, BLOCK, 2 * DH
    )
    library_back = jnp.concatenate([window, global_pairs, refetched], axis=0)

    def backward_step(inputs):
        query_block, gradient_tile, out_block, logsum, spots, allowed_row = inputs
        keys_here, values_here = key_rows(library_back, spots)
        factor = DH ** (-0.5)
        scores = masked_scores(query_block, keys_here, allowed_row)
        probs = jnp.exp(scores - logsum)
        probs16 = probs.astype(jnp.bfloat16)
        delta = jnp.sum(gradient_tile.astype(jnp.float32) * out_block.astype(jnp.float32), axis=-1)
        dprobs = jnp.einsum(
            "thd,kd->htk", gradient_tile, values_here, preferred_element_type=jnp.float32
        )
        dscores = (probs * (dprobs - jnp.transpose(delta)[:, :, None])).astype(jnp.bfloat16)
        dquery = (
            jnp.einsum("htk,kd->thd", dscores, keys_here, preferred_element_type=jnp.float32)
            * factor
        )
        dkey = (
            jnp.einsum("htk,thd->kd", dscores, query_block, preferred_element_type=jnp.float32)
            * factor
        )
        dvalue = jnp.einsum(
            "htk,thd->kd", probs16, gradient_tile, preferred_element_type=jnp.float32
        )
        terms = jnp.concatenate([dkey, dvalue], axis=1).reshape(spots.shape[0], BLOCK, 2 * DH)
        return (dquery.astype(jnp.bfloat16), terms)

    dquery_blocks, terms = lax.map(
        backward_step, (query_blocks, grad_blocks, out_blocks, logsums, positions, allowed)
    )
    attn_out = out_blocks.reshape(tok_count, heads_here * DH)
    d_queries = dquery_blocks.reshape(tok_count, heads_here * DH)
    prev_terms = terms[:, 0]
    self_terms = terms[:, 1]
    next_terms = terms[:, 2]
    zero_block = jnp.zeros((1, BLOCK, 2 * DH), jnp.float32)
    grads = (
        self_terms
        + jnp.concatenate([prev_terms[1:], zero_block], axis=0)
        + jnp.concatenate([zero_block, next_terms[:-1]], axis=0)
    )
    rims = jnp.concatenate([prev_terms[0], next_terms[-1]], axis=0).astype(jnp.bfloat16)
    arrived = padded_2(rims, (("seq", 0),), BLOCK)
    from_left = arrived[:BLOCK].astype(jnp.float32)
    from_right = arrived[3 * BLOCK :].astype(jnp.float32)
    edge_first = jnp.concatenate(
        [from_left[None], jnp.zeros((blocks_here - 1, BLOCK, 2 * DH), jnp.float32)], axis=0
    )
    edge_last = jnp.concatenate(
        [jnp.zeros((blocks_here - 1, BLOCK, 2 * DH), jnp.float32), from_right[None]], axis=0
    )
    grads = grads + edge_first + edge_last
    global_terms = jnp.sum(terms[:, 3 : 3 + GLOB], axis=0)
    global_total = lax.psum(global_terms, "seq")
    global_hits = ((glob_blocks // blocks_here)[:, None] == here) & (
        (glob_blocks % blocks_here)[:, None] == block_ids[None, :]
    )
    grads = grads + jnp.sum(
        jnp.where(global_hits[:, :, None, None], global_total[:, None], 0.0), axis=0
    )
    random_terms = terms[:, 3 + GLOB :].reshape(entry_count, BLOCK * 2 * DH).astype(jnp.bfloat16)
    outgoing = jnp.dot(
        placing.astype(jnp.bfloat16), random_terms, preferred_element_type=jnp.float32
    ).astype(jnp.bfloat16)
    returned = lax.all_to_all(
        outgoing.reshape(seq_count, capacity, BLOCK, 2 * DH),
        "seq",
        split_axis=0,
        concat_axis=0,
        tiled=True,
    )
    landing = (incoming[None, :] == block_ids[:, None]).astype(jnp.bfloat16)
    grads = grads + jnp.dot(
        landing,
        returned.reshape(position_count, BLOCK * 2 * DH),
        preferred_element_type=jnp.float32,
    ).reshape(blocks_here, BLOCK, 2 * DH)
    packed = grads.astype(jnp.bfloat16).reshape(tok_count, 1, 2 * DH)
    restored = lax.all_to_all(packed, "head", split_axis=0, concat_axis=1, tiled=True)
    d_keys = restored[:, :, :DH].reshape(short, KVH * DH)
    d_values = restored[:, :, DH:].reshape(short, KVH * DH)
    return (attn_out, d_queries, d_keys, d_values)


def flips(count, bits):
    return [(i, i ^ bits) for i in range(count)]


def head_columns(head, offset):
    return pl.ds(pl.multiple_of((head ^ offset) * DH, DH), DH)


def run_copies(copies):
    for copy in copies:
        copy.start()
    for copy in copies:
        copy.wait()


def pack_kernel(*refs):
    keys_ref, values_ref, *piece_refs, sems = refs
    head = lax.axis_index("head")
    short = keys_ref.shape[0]
    moves = []
    for offset, piece in enumerate(piece_refs):
        columns = head_columns(head, offset)
        moves.append((keys_ref.at[:, columns], piece.at[pl.ds(0, short)]))
        moves.append((values_ref.at[:, columns], piece.at[pl.ds(short, short)]))
    run_copies([pltpu.make_async_copy(a, b, sems.at[n]) for n, (a, b) in enumerate(moves)])


def unpack_kernel(*refs):
    piece_refs, (keys_ref, values_ref) = refs[:-2], refs[-2:]
    head = lax.axis_index("head")
    short = keys_ref.shape[0]
    for offset, piece in enumerate(piece_refs):
        columns = head_columns(head, offset)
        keys_ref[:, columns] = piece[:short, :]
        values_ref[:, columns] = piece[short:, :]


def dot(left, right, left_dim, right_dim):
    return lax.dot_general(
        left,
        right,
        (((left_dim,), (right_dim,)), ((), ())),
        preferred_element_type=jnp.float32,
    )


def listed_spots(spots_ref, step):
    return [spots_ref[step, number] for number in range(spots_ref.shape[1])]


def begin(part_refs, starts, library, total):
    for part, at in zip(part_refs, starts):
        library[at : at + part.shape[0]] = part[...]
    total[...] = jnp.zeros_like(total)


def add_terms(total, spots, terms):
    for number, spot in enumerate(spots):
        total[spot] += terms[number * BLOCK : (number + 1) * BLOCK]


def finish(total, keep_ref, ship_ref):
    pairs, size = keep_ref.shape[:2]
    for pair in range(pairs):
        keep_ref[pair] = total[pl.ds(2 * pair * size, size)]
        ship_ref[pair] = total[pl.ds((2 * pair + 1) * size, size)].astype(jnp.bfloat16)


def stacked_heads(ref, step, chunk):
    rows = slice(step * BLOCK, (step + 1) * BLOCK)
    return jnp.concatenate([ref[rows, h * DH : (h + 1) * DH] for h in chunk], axis=0)


def chunks_of(heads, size):
    return [range(start, start + size) for start in range(0, heads, size)]


def list_entries(spots_ref, rand_ref, glob_ref, seq_count):
    here = lax.axis_index("seq")
    head = lax.axis_index("head")
    blocks_here = rand_ref.shape[0]
    last = seq_count * blocks_here - 1
    for step in range(blocks_here):
        block = here * blocks_here + step
        names = [jnp.maximum(block - 1, 0), block, jnp.minimum(block + 1, last)]
        names += [glob_ref[i] for i in range(GLOB)]
        names += [rand_ref[step, i] for i in range(RAND)]
        for number, name in enumerate(names):
            owner = lax.div(name, blocks_here) ^ here
            spots_ref[step, number] = owner * blocks_here + (lax.rem(name, blocks_here) ^ head)


def probs_kernel(seq_count, starts, size, *refs):
    sources, part_refs, refs = refs[:4], refs[4 : 4 + seq_count], refs[4 + seq_count :]
    probs_ref, rows_ref, keep_ref, ship_ref, spots_ref, query_ref, grad_ref = refs[:7]
    library, total, rand_ref, glob_ref, sems = refs[7:]
    targets = (rand_ref, glob_ref, query_ref, grad_ref)
    moves = enumerate(zip(sources, targets))
    copies = [pltpu.make_async_copy(a, b, sems.at[n]) for n, (a, b) in moves]
    for copy in copies:
        copy.start()
    blocks_here = probs_ref.shape[0]
    all_blocks = library.shape[0]
    begin(part_refs, starts, library, total)
    copies[0].wait()
    copies[1].wait()
    list_entries(spots_ref, rand_ref, glob_ref, seq_count)
    copies[2].wait()
    copies[3].wait()
    for step in range(blocks_here):
        block = lax.axis_index("seq") * blocks_here + step
        spots = listed_spots(spots_ref, step)
        for number, spot in enumerate(spots):
            rows_ref[step, pl.ds(number * BLOCK, BLOCK), :] = library[spot]
        first_bias = jnp.where(block == 0, NEG_FILL, 0.0)
        last_bias = jnp.where(block == all_blocks - 1, NEG_FILL, 0.0)
        scale = DH ** (-0.5) * math.log2(math.e)
        terms = 0.0
        for chunk in chunks_of(query_ref.shape[1] // DH, size):
            query = stacked_heads(query_ref, step, chunk)
            grad = stacked_heads(grad_ref, step, chunk)
            scores = dot(rows_ref[step], query, 1, 1)
            scores = jnp.concatenate(
                [
                    scores[:BLOCK] + first_bias,
                    scores[BLOCK : 2 * BLOCK],
                    scores[2 * BLOCK : 3 * BLOCK] + last_bias,
                    scores[3 * BLOCK :],
                ],
                axis=0,
            )
            peak = jnp.max(scores, axis=0, keepdims=True)
            weights = jnp.exp2((scores - peak) * scale)
            probs = weights * (1.0 / jnp.sum(weights, axis=0, keepdims=True))
            probs16 = probs.astype(jnp.bfloat16)
            probs_ref[step, :, chunk[0] * BLOCK : (chunk[-1] + 1) * BLOCK] = probs16
            terms = terms + dot(probs16, grad, 1, 0)
        add_terms(total, spots, terms)
    finish(total, keep_ref, ship_ref)


def send_tile(stage, out_ref, step, sems):
    rows = pl.ds(step * BLOCK, BLOCK)
    copy = pltpu.make_async_copy(stage.at[step], out_ref.at[rows], sems.at[step])
    copy.start()
    return copy


def dscores_kernel(starts, size, *refs):
    spots_ref, query_ref, grad_ref, probs_ref = refs[:4]
    part_refs, refs = refs[4:-9], refs[-9:]
    out_ref, dscores_ref, keep_ref, ship_ref, library, total, rows_ref, stage, sems = refs
    begin(part_refs, starts, library, total)
    copies = []
    for step in range(stage.shape[0]):
        spots = listed_spots(spots_ref, step)
        for number, spot in enumerate(spots):
            rows_ref[step, pl.ds(number * BLOCK, BLOCK), :] = library[spot]
        terms = 0.0
        for chunk in chunks_of(query_ref.shape[1] // DH, size):
            columns = slice(chunk[0] * BLOCK, (chunk[-1] + 1) * BLOCK)
            query = stacked_heads(query_ref, step, chunk)
            grad = stacked_heads(grad_ref, step, chunk)
            probs16 = probs_ref[step, :, columns]
            result = dot(rows_ref[step], probs16, 0, 0).astype(jnp.bfloat16).astype(jnp.float32)
            grad_across = jnp.transpose(grad.astype(jnp.float32))
            delta = jnp.sum(grad_across * result, axis=0, keepdims=True)
            dprobs = dot(rows_ref[step], grad, 1, 1)
            dscores = (probs16.astype(jnp.float32) * (dprobs - delta)).astype(jnp.bfloat16)
            dscores_ref[step, :, columns] = dscores
            terms = terms + dot(dscores, query, 1, 0)
            down = jnp.transpose(result).astype(jnp.bfloat16)
            for number, h in enumerate(chunk):
                stage[step, :, h * DH : (h + 1) * DH] = down[number * BLOCK : (number + 1) * BLOCK]
        add_terms(total, spots, terms * DH ** (-0.5))
        copies.append(send_tile(stage, out_ref, step, sems))
    finish(total, keep_ref, ship_ref)
    for copy in copies:
        copy.wait()


def dquery_kernel(size, dscores_ref, rows_ref, dquery_ref, stage, sems):
    copies = []
    for step in range(stage.shape[0]):
        for chunk in chunks_of(dquery_ref.shape[1] // DH, size):
            columns = slice(chunk[0] * BLOCK, (chunk[-1] + 1) * BLOCK)
            across = dot(rows_ref[step], dscores_ref[step, :, columns], 0, 0) * DH ** (-0.5)
            down = jnp.transpose(across).astype(jnp.bfloat16)
            for number, h in enumerate(chunk):
                rows = slice(number * BLOCK, (number + 1) * BLOCK)
                stage[step, :, h * DH : (h + 1) * DH] = down[rows]
        copies.append(send_tile(stage, dquery_ref, step, sems))
    for copy in copies:
        copy.wait()


def small_grant():
    return pltpu.CompilerParams(vmem_limit_bytes=8 * 1024 * 1024)


def kernel_options(products, pairs):
    return {
        "compiler_params": pltpu.CompilerParams(vmem_limit_bytes=36 * 1024 * 1024),
        "cost_estimate": pl.CostEstimate(
            flops=4 * products * pairs * DH, bytes_accessed=4 * pairs, transcendentals=pairs
        ),
    }


def whole_body(queries, keys, values, d_out, rand_blocks, glob_blocks):
    seq_count = lax.axis_size("seq")
    head_count = lax.axis_size("head")
    short = keys.shape[0]
    tok_count, width = queries.shape
    heads_here = width // DH
    blocks_here = tok_count // BLOCK
    pair_count = seq_count // 2
    listed = (3 + GLOB + RAND) * BLOCK
    columns = heads_here * BLOCK
    pairs = blocks_here * listed * columns
    size = heads_here

    smem = pl.BlockSpec(memory_space=pltpu.SMEM)
    anywhere = pl.BlockSpec(memory_space=pl.ANY)
    tile_shape = jax.ShapeDtypeStruct(queries.shape, jnp.bfloat16)
    piece = jax.ShapeDtypeStruct((2 * short, DH), jnp.bfloat16)
    spots_shape = jax.ShapeDtypeStruct((blocks_here, 3 + GLOB + RAND), jnp.int32)
    rand_blocks, glob_blocks, keys, values, queries, d_out = [
        pltpu.with_memory_space_constraint(x, pltpu.HBM)
        for x in (rand_blocks, glob_blocks, keys, values, queries, d_out)
    ]
    pieces = pl.pallas_call(
        pack_kernel,
        in_specs=[anywhere] * 2,
        out_specs=[anywhere] * head_count,
        out_shape=[piece] * head_count,
        scratch_shapes=[pltpu.SemaphoreType.DMA((2 * head_count,))],
        compiler_params=small_grant(),
    )(keys, values)
    pieces = [pieces[0]] + [
        lax.ppermute(pieces[k], "head", flips(head_count, k)) for k in range(1, head_count)
    ]

    def along_far(own):
        parts = [own]
        for k in range(2, seq_count, 2):
            parts.append(lax.ppermute(own, "seq", flips(seq_count, k)))
        return parts

    def to_near(part):
        return lax.ppermute(part, "seq", flips(seq_count, 1))

    key_far = along_far(jnp.stack([p[:short] for p in pieces]))
    order = sorted(range(pair_count), key=lambda n: (bin(n).count("1"), -n))
    key_parts = [part for n in order for part in (key_far[n], to_near(key_far[n]))]
    key_starts = [slot * blocks_here for n in order for slot in (2 * n, 2 * n + 1)]
    value_starts = [2 * n * blocks_here for n in order]
    value_own = jnp.stack([p[short:] for p in pieces])
    value_pair = jnp.concatenate([value_own, to_near(value_own)])
    value_pair, _ = lax.optimization_barrier((value_pair, key_far[1:]))
    value_far = along_far(value_pair)
    value_parts = [value_far[n] for n in order]

    lists = pltpu.VMEM((blocks_here, listed, DH), jnp.bfloat16)
    stage = pltpu.VMEM((blocks_here, BLOCK, width), jnp.bfloat16)
    tile_sems = pltpu.SemaphoreType.DMA((blocks_here,))
    vmem = pl.BlockSpec(memory_space=pltpu.VMEM)
    half = (pair_count, blocks_here, BLOCK, DH)
    square_shape = jax.ShapeDtypeStruct((blocks_here, listed, columns), jnp.bfloat16)
    listing_shape = jax.ShapeDtypeStruct((blocks_here, listed, DH), jnp.bfloat16)
    keep_shape = jax.ShapeDtypeStruct(half, jnp.float32)
    ship_shape = jax.ShapeDtypeStruct(half, jnp.bfloat16)
    library = pltpu.VMEM((seq_count * blocks_here, BLOCK, DH), jnp.bfloat16)
    total = pltpu.VMEM((seq_count * blocks_here, BLOCK, DH), jnp.float32)

    probs, key_lists, value_keep, value_ship, spots, query_here, grad_here = pl.pallas_call(
        lambda *refs: probs_kernel(seq_count, key_starts, size, *refs),
        in_specs=[anywhere] * 4 + [vmem] * len(key_parts),
        out_specs=[vmem] * 4 + [smem] + [vmem] * 2,
        out_shape=[
            square_shape,
            listing_shape,
            keep_shape,
            ship_shape,
            spots_shape,
            tile_shape,
            tile_shape,
        ],
        scratch_shapes=[
            library,
            total,
            pltpu.SMEM(rand_blocks.shape, jnp.int32),
            pltpu.SMEM(glob_blocks.shape, jnp.int32),
            pltpu.SemaphoreType.DMA((4,)),
        ],
        **kernel_options(2, pairs),
    )(rand_blocks, glob_blocks, queries, d_out, *key_parts)
    value_near = lax.ppermute(value_ship, "seq", flips(seq_count, 1))
    attn_out, dscores, key_keep, key_ship = pl.pallas_call(
        lambda *refs: dscores_kernel(value_starts, size, *refs),
        in_specs=[smem, vmem, vmem, vmem] + [vmem] * len(value_parts),
        out_specs=[anywhere, vmem, vmem, vmem],
        out_shape=[tile_shape, square_shape, keep_shape, ship_shape],
        scratch_shapes=[library, total, lists, stage, tile_sems],
        **kernel_options(3, pairs),
    )(spots, query_here, grad_here, probs, *value_parts)
    key_near = lax.ppermute(key_ship, "seq", flips(seq_count, 1))

    def sums_of(keep, near):
        sums = keep + near.astype(jnp.float32)
        return sums[0], [sums[pair].astype(jnp.bfloat16) for pair in range(1, pair_count)]

    def from_far(sums):
        return [
            lax.ppermute(sums[pair - 1], "seq", flips(seq_count, 2 * pair))
            for pair in order[1:]
        ]

    def added(own, far):
        for part in far:
            own = own + part.astype(jnp.float32)
        return own

    key_own, key_sums = sums_of(key_keep, key_near)
    key_far = from_far(key_sums)
    value_own, value_sums = sums_of(value_keep, value_near)
    value_terms = from_far(value_sums)
    d_queries = pl.pallas_call(
        lambda *refs: dquery_kernel(size, *refs),
        in_specs=[vmem, vmem],
        out_specs=anywhere,
        out_shape=tile_shape,
        scratch_shapes=[stage, tile_sems],
        **kernel_options(1, pairs),
    )(*lax.optimization_barrier((dscores, key_lists, key_sums))[:2])

    key_far, value_terms, d_queries = lax.optimization_barrier((key_far, value_terms, d_queries))
    packed = jnp.concatenate(
        [added(key_own, key_far), added(value_own, value_terms)], axis=1
    ).astype(jnp.bfloat16)
    back = [packed[0]] + [
        lax.ppermute(packed[k], "head", flips(head_count, k)) for k in range(1, head_count)
    ]
    flat = jax.ShapeDtypeStruct(keys.shape, jnp.bfloat16)
    d_keys, d_values = pl.pallas_call(
        unpack_kernel, out_shape=[flat, flat], compiler_params=small_grant()
    )(*back)
    return (attn_out, d_queries, d_keys, d_values)


def body(queries, keys, values, d_out, rand_blocks, glob_blocks):
    seq_count = lax.axis_size("seq")
    head_count = lax.axis_size("head")
    blocks_here = rand_blocks.shape[0]
    capacity = -(-rand_blocks.size // seq_count)
    powers = all(n & (n - 1) == 0 for n in (seq_count, head_count))
    fits = keys.shape[0] == BLOCK and blocks_here == head_count
    if capacity >= blocks_here and seq_count > 1 and powers and fits:
        return whole_body(queries, keys, values, d_out, rand_blocks, glob_blocks)
    return request_body(queries, keys, values, d_out, rand_blocks, glob_blocks)


def solution(mesh):
    in_specs = (
        P("seq", "head"),
        P(("seq", "head"), None),
        P(("seq", "head"), None),
        P("seq", "head"),
        P("seq", None),
        P(),
    )
    out_specs = (
        P("seq", "head"),
        P("seq", "head"),
        P(("seq", "head"), None),
        P(("seq", "head"), None),
    )
    return jax.shard_map(body, mesh=mesh, in_specs=in_specs, out_specs=out_specs, check_vma=False)
```

```python
import math

import jax
import jax.numpy as jnp
from jax import lax
from jax.experimental import pallas as pl
from jax.experimental.pallas import tpu as pltpu
from jax.sharding import PartitionSpec as P

DH = 128
KVH = 4
BLOCK = 64
GLOB = 2
RAND = 8


NEG_FILL = -1e30


def padded_2(cells, sides, width):
    for axis, dim in sides:
        count = lax.axis_size(axis)
        ends = count - 1
        head = lax.slice_in_dim(cells, 0, width, axis=dim)
        tail = lax.slice_in_dim(cells, cells.shape[dim] - width, cells.shape[dim], axis=dim)
        cells = jnp.concatenate(
            [
                lax.ppermute(tail, axis, [(i, (i + 1) % count) for i in range(ends)]),
                cells,
                lax.ppermute(head, axis, [((i + 1) % count, i) for i in range(ends)]),
            ],
            axis=dim,
        )
    return cells


def broadcast(block, axis, source):
    block = jnp.where(lax.axis_index(axis) == source, block, jnp.zeros_like(block))
    return lax.psum(block, axis)


def key_rows(library, spots):
    chosen = jnp.stack(
        [
            lax.dynamic_index_in_dim(library, spots[i], 0, keepdims=False)
            for i in range(spots.shape[0])
        ]
    )
    flat = chosen.reshape(chosen.shape[0] * chosen.shape[1], chosen.shape[2])
    return (flat[:, :DH], flat[:, DH:])


def masked_scores(query_block, keys_here, allowed_row):
    factor = DH ** (-0.5)
    scores = (
        jnp.einsum("thd,kd->htk", query_block, keys_here, preferred_element_type=jnp.float32)
        * factor
    )
    widened = jnp.repeat(allowed_row, keys_here.shape[0] // allowed_row.shape[0])
    return jnp.where(widened[None, None, :], scores, NEG_FILL)


def request_body(queries, keys, values, d_out, rand_blocks, glob_blocks):
    seq_count = lax.axis_size("seq")
    here = lax.axis_index("seq")
    short = keys.shape[0]
    stacked = jnp.concatenate(
        [keys.reshape(short, KVH, DH), values.reshape(short, KVH, DH)], axis=2
    )
    mine = lax.all_to_all(stacked, "head", split_axis=1, concat_axis=0, tiled=True)
    tok_count = mine.shape[0]
    blocks_here = tok_count // BLOCK
    flat_pairs = mine.reshape(tok_count, 2 * DH)
    own_blocks = flat_pairs.reshape(blocks_here, BLOCK, 2 * DH)
    padded = padded_2(flat_pairs, (("seq", 0),), BLOCK)
    window = padded.reshape(blocks_here + 2, BLOCK, 2 * DH)
    global_parts = []
    for number in range(GLOB):
        target = glob_blocks[number]
        piece = lax.dynamic_index_in_dim(own_blocks, target % blocks_here, 0, keepdims=False)
        global_parts.append(broadcast(piece, "seq", target // blocks_here))
    global_pairs = jnp.stack(global_parts)
    entries = rand_blocks.reshape(-1)
    entry_count = entries.shape[0]
    capacity = -(-entry_count // seq_count)
    position_count = seq_count * capacity
    owners = entries // blocks_here
    inner_index = entries % blocks_here
    order = jnp.arange(entry_count, dtype=jnp.int32)
    earlier = (owners[:, None] == owners[None, :]) & (order[:, None] > order[None, :])
    ranks = jnp.sum(earlier.astype(jnp.int32), axis=1)
    slots = owners * capacity + ranks
    placing = slots[None, :] == jnp.arange(position_count, dtype=jnp.int32)[:, None]
    wanted = jnp.sum(jnp.where(placing, inner_index[None, :], 0), axis=1).reshape(
        seq_count, capacity
    )
    incoming = lax.all_to_all(wanted, "seq", split_axis=0, concat_axis=0, tiled=True).reshape(
        position_count
    )
    block_ids = jnp.arange(blocks_here, dtype=jnp.int32)
    picking = (incoming[:, None] == block_ids[None, :]).astype(jnp.bfloat16)
    served = (
        jnp.dot(
            picking,
            own_blocks.reshape(blocks_here, BLOCK * 2 * DH),
            preferred_element_type=jnp.float32,
        )
        .astype(jnp.bfloat16)
        .reshape(seq_count, capacity, BLOCK, 2 * DH)
    )
    fetched = lax.all_to_all(served, "seq", split_axis=0, concat_axis=0, tiled=True).reshape(
        position_count, BLOCK, 2 * DH
    )
    window_ids = jnp.stack([block_ids, block_ids + 1, block_ids + 2], axis=1)
    global_ids = jnp.broadcast_to(
        blocks_here + 2 + jnp.arange(GLOB, dtype=jnp.int32), (blocks_here, GLOB)
    )
    random_ids = blocks_here + 2 + GLOB + slots.reshape(blocks_here, RAND)
    positions = jnp.concatenate([window_ids, global_ids, random_ids], axis=1)
    allowed = jnp.concatenate(
        [
            jnp.logical_not((block_ids == 0) & (here == 0))[:, None],
            jnp.ones((blocks_here, 1), jnp.bool_),
            jnp.logical_not((block_ids == blocks_here - 1) & (here == seq_count - 1))[:, None],
            jnp.ones((blocks_here, GLOB + RAND), jnp.bool_),
        ],
        axis=1,
    )
    library = jnp.concatenate([window, global_pairs, fetched], axis=0)
    heads_here = queries.shape[1] // DH
    query_blocks = queries.reshape(blocks_here, BLOCK, heads_here, DH)
    grad_blocks = d_out.reshape(blocks_here, BLOCK, heads_here, DH)

    def forward_step(inputs):
        query_block, spots, allowed_row = inputs
        keys_here, values_here = key_rows(library, spots)
        scores = masked_scores(query_block, keys_here, allowed_row)
        peak = jnp.max(scores, axis=-1, keepdims=True)
        logsum = peak + jnp.log(jnp.sum(jnp.exp(scores - peak), axis=-1, keepdims=True))
        probs16 = jnp.exp(scores - logsum).astype(jnp.bfloat16)
        result = jnp.einsum("htk,kd->thd", probs16, values_here, preferred_element_type=jnp.float32)
        return (result.astype(jnp.bfloat16), logsum)

    out_blocks, logsums = lax.map(forward_step, (query_blocks, positions, allowed))
    refetched = lax.all_to_all(served, "seq", split_axis=0, concat_axis=0, tiled=True).reshape(
        position_count, BLOCK, 2 * DH
    )
    library_back = jnp.concatenate([window, global_pairs, refetched], axis=0)

    def backward_step(inputs):
        query_block, gradient_tile, out_block, logsum, spots, allowed_row = inputs
        keys_here, values_here = key_rows(library_back, spots)
        factor = DH ** (-0.5)
        scores = masked_scores(query_block, keys_here, allowed_row)
        probs = jnp.exp(scores - logsum)
        probs16 = probs.astype(jnp.bfloat16)
        delta = jnp.sum(gradient_tile.astype(jnp.float32) * out_block.astype(jnp.float32), axis=-1)
        dprobs = jnp.einsum(
            "thd,kd->htk", gradient_tile, values_here, preferred_element_type=jnp.float32
        )
        dscores = (probs * (dprobs - jnp.transpose(delta)[:, :, None])).astype(jnp.bfloat16)
        dquery = (
            jnp.einsum("htk,kd->thd", dscores, keys_here, preferred_element_type=jnp.float32)
            * factor
        )
        dkey = (
            jnp.einsum("htk,thd->kd", dscores, query_block, preferred_element_type=jnp.float32)
            * factor
        )
        dvalue = jnp.einsum(
            "htk,thd->kd", probs16, gradient_tile, preferred_element_type=jnp.float32
        )
        terms = jnp.concatenate([dkey, dvalue], axis=1).reshape(spots.shape[0], BLOCK, 2 * DH)
        return (dquery.astype(jnp.bfloat16), terms)

    dquery_blocks, terms = lax.map(
        backward_step, (query_blocks, grad_blocks, out_blocks, logsums, positions, allowed)
    )
    attn_out = out_blocks.reshape(tok_count, heads_here * DH)
    d_queries = dquery_blocks.reshape(tok_count, heads_here * DH)
    prev_terms = terms[:, 0]
    self_terms = terms[:, 1]
    next_terms = terms[:, 2]
    zero_block = jnp.zeros((1, BLOCK, 2 * DH), jnp.float32)
    grads = (
        self_terms
        + jnp.concatenate([prev_terms[1:], zero_block], axis=0)
        + jnp.concatenate([zero_block, next_terms[:-1]], axis=0)
    )
    rims = jnp.concatenate([prev_terms[0], next_terms[-1]], axis=0).astype(jnp.bfloat16)
    arrived = padded_2(rims, (("seq", 0),), BLOCK)
    from_left = arrived[:BLOCK].astype(jnp.float32)
    from_right = arrived[3 * BLOCK :].astype(jnp.float32)
    edge_first = jnp.concatenate(
        [from_left[None], jnp.zeros((blocks_here - 1, BLOCK, 2 * DH), jnp.float32)], axis=0
    )
    edge_last = jnp.concatenate(
        [jnp.zeros((blocks_here - 1, BLOCK, 2 * DH), jnp.float32), from_right[None]], axis=0
    )
    grads = grads + edge_first + edge_last
    global_terms = jnp.sum(terms[:, 3 : 3 + GLOB], axis=0)
    global_total = lax.psum(global_terms, "seq")
    global_hits = ((glob_blocks // blocks_here)[:, None] == here) & (
        (glob_blocks % blocks_here)[:, None] == block_ids[None, :]
    )
    grads = grads + jnp.sum(
        jnp.where(global_hits[:, :, None, None], global_total[:, None], 0.0), axis=0
    )
    random_terms = terms[:, 3 + GLOB :].reshape(entry_count, BLOCK * 2 * DH).astype(jnp.bfloat16)
    outgoing = jnp.dot(
        placing.astype(jnp.bfloat16), random_terms, preferred_element_type=jnp.float32
    ).astype(jnp.bfloat16)
    returned = lax.all_to_all(
        outgoing.reshape(seq_count, capacity, BLOCK, 2 * DH),
        "seq",
        split_axis=0,
        concat_axis=0,
        tiled=True,
    )
    landing = (incoming[None, :] == block_ids[:, None]).astype(jnp.bfloat16)
    grads = grads + jnp.dot(
        landing,
        returned.reshape(position_count, BLOCK * 2 * DH),
        preferred_element_type=jnp.float32,
    ).reshape(blocks_here, BLOCK, 2 * DH)
    packed = grads.astype(jnp.bfloat16).reshape(tok_count, 1, 2 * DH)
    restored = lax.all_to_all(packed, "head", split_axis=0, concat_axis=1, tiled=True)
    d_keys = restored[:, :, :DH].reshape(short, KVH * DH)
    d_values = restored[:, :, DH:].reshape(short, KVH * DH)
    return (attn_out, d_queries, d_keys, d_values)


def flips(count, bits):
    return [(i, i ^ bits) for i in range(count)]


def head_order(count):
    return [n ^ (n >> 1) for n in range(count)]


def head_columns(head, offset):
    return pl.ds(pl.multiple_of((head ^ offset) * DH, DH), DH)


def run_copies(copies):
    for copy in copies:
        copy.start()
    for copy in copies:
        copy.wait()


def pack_kernel(*refs):
    keys_ref, values_ref, *piece_refs, sems = refs
    head = lax.axis_index("head")
    short = keys_ref.shape[0]
    moves = []
    for offset, piece in enumerate(piece_refs):
        columns = head_columns(head, offset)
        moves.append((keys_ref.at[:, columns], piece.at[pl.ds(0, short)]))
        moves.append((values_ref.at[:, columns], piece.at[pl.ds(short, short)]))
    run_copies([pltpu.make_async_copy(a, b, sems.at[n]) for n, (a, b) in enumerate(moves)])


def unpack_kernel(*refs):
    piece_refs, (keys_ref, values_ref) = refs[:-2], refs[-2:]
    head = lax.axis_index("head")
    short = keys_ref.shape[0]
    for offset, piece in zip(head_order(len(piece_refs)), piece_refs):
        columns = head_columns(head, offset)
        keys_ref[:, columns] = piece[:short, :]
        values_ref[:, columns] = piece[short:, :]


def dot(left, right, left_dim, right_dim):
    return lax.dot_general(
        left,
        right,
        (((left_dim,), (right_dim,)), ((), ())),
        preferred_element_type=jnp.float32,
    )


def listed_spots(spots_ref, step):
    return [spots_ref[step, number] for number in range(spots_ref.shape[1])]


def begin(part_refs, starts, library, total):
    for part, at in zip(part_refs, starts):
        library[at : at + part.shape[0]] = part[...]
    total[...] = jnp.zeros_like(total)


def add_terms(total, spots, terms):
    for number, spot in enumerate(spots):
        total[spot] += terms[number * BLOCK : (number + 1) * BLOCK]


def finish(total, keep_ref, ship_ref):
    pairs, size = keep_ref.shape[:2]
    for pair in range(pairs):
        keep_ref[pair] = total[pl.ds(2 * pair * size, size)]
        ship_ref[pair] = total[pl.ds((2 * pair + 1) * size, size)].astype(jnp.bfloat16)


def stacked_heads(ref, step, chunk):
    rows = slice(step * BLOCK, (step + 1) * BLOCK)
    return jnp.concatenate([ref[rows, h * DH : (h + 1) * DH] for h in chunk], axis=0)


def chunks_of(heads, size):
    return [range(start, start + size) for start in range(0, heads, size)]


def list_entries(spots_ref, rand_ref, glob_ref, seq_count):
    here = lax.axis_index("seq")
    head = lax.axis_index("head")
    blocks_here = rand_ref.shape[0]
    last = seq_count * blocks_here - 1
    for step in range(blocks_here):
        block = here * blocks_here + step
        names = [jnp.maximum(block - 1, 0), block, jnp.minimum(block + 1, last)]
        names += [glob_ref[i] for i in range(GLOB)]
        names += [rand_ref[step, i] for i in range(RAND)]
        for number, name in enumerate(names):
            owner = lax.div(name, blocks_here) ^ here
            spots_ref[step, number] = owner * blocks_here + (lax.rem(name, blocks_here) ^ head)


def probs_kernel(seq_count, starts, size, *refs):
    sources, part_refs, refs = refs[:4], refs[4 : 4 + seq_count], refs[4 + seq_count :]
    probs_ref, rows_ref, keep_ref, ship_ref, spots_ref, query_ref, grad_ref = refs[:7]
    library, total, rand_ref, glob_ref, sems = refs[7:]
    targets = (rand_ref, glob_ref, query_ref, grad_ref)
    moves = enumerate(zip(sources, targets))
    copies = [pltpu.make_async_copy(a, b, sems.at[n]) for n, (a, b) in moves]
    for copy in copies:
        copy.start()
    blocks_here = probs_ref.shape[0]
    all_blocks = library.shape[0]
    begin(part_refs, starts, library, total)
    copies[0].wait()
    copies[1].wait()
    list_entries(spots_ref, rand_ref, glob_ref, seq_count)
    copies[2].wait()
    copies[3].wait()
    for step in range(blocks_here):
        block = lax.axis_index("seq") * blocks_here + step
        spots = listed_spots(spots_ref, step)
        for number, spot in enumerate(spots):
            rows_ref[step, pl.ds(number * BLOCK, BLOCK), :] = library[spot]
        first_bias = jnp.where(block == 0, NEG_FILL, 0.0)
        last_bias = jnp.where(block == all_blocks - 1, NEG_FILL, 0.0)
        scale = DH ** (-0.5) * math.log2(math.e)
        terms = 0.0
        for chunk in chunks_of(query_ref.shape[1] // DH, size):
            query = stacked_heads(query_ref, step, chunk)
            grad = stacked_heads(grad_ref, step, chunk)
            scores = dot(rows_ref[step], query, 1, 1)
            scores = jnp.concatenate(
                [
                    scores[:BLOCK] + first_bias,
                    scores[BLOCK : 2 * BLOCK],
                    scores[2 * BLOCK : 3 * BLOCK] + last_bias,
                    scores[3 * BLOCK :],
                ],
                axis=0,
            )
            peak = jnp.max(scores, axis=0, keepdims=True)
            weights = jnp.exp2((scores - peak) * scale)
            probs = weights * (1.0 / jnp.sum(weights, axis=0, keepdims=True))
            probs16 = probs.astype(jnp.bfloat16)
            probs_ref[step, :, chunk[0] * BLOCK : (chunk[-1] + 1) * BLOCK] = probs16
            terms = terms + dot(probs16, grad, 1, 0)
        add_terms(total, spots, terms)
    finish(total, keep_ref, ship_ref)


def send_tile(stage, out_ref, step, sems):
    rows = pl.ds(step * BLOCK, BLOCK)
    copy = pltpu.make_async_copy(stage.at[step], out_ref.at[rows], sems.at[step])
    copy.start()
    return copy


def dscores_kernel(starts, size, *refs):
    spots_ref, query_ref, grad_ref, probs_ref = refs[:4]
    part_refs, refs = refs[4:-9], refs[-9:]
    out_ref, dscores_ref, keep_ref, ship_ref, library, total, rows_ref, stage, sems = refs
    begin(part_refs, starts, library, total)
    copies = []
    for step in range(stage.shape[0]):
        spots = listed_spots(spots_ref, step)
        for number, spot in enumerate(spots):
            rows_ref[step, pl.ds(number * BLOCK, BLOCK), :] = library[spot]
        terms = 0.0
        for chunk in chunks_of(query_ref.shape[1] // DH, size):
            columns = slice(chunk[0] * BLOCK, (chunk[-1] + 1) * BLOCK)
            query = stacked_heads(query_ref, step, chunk)
            grad = stacked_heads(grad_ref, step, chunk)
            probs16 = probs_ref[step, :, columns]
            result = dot(rows_ref[step], probs16, 0, 0).astype(jnp.bfloat16).astype(jnp.float32)
            grad_across = jnp.transpose(grad.astype(jnp.float32))
            delta = jnp.sum(grad_across * result, axis=0, keepdims=True)
            dprobs = dot(rows_ref[step], grad, 1, 1)
            dscores = (probs16.astype(jnp.float32) * (dprobs - delta)).astype(jnp.bfloat16)
            dscores_ref[step, :, columns] = dscores
            terms = terms + dot(dscores, query, 1, 0)
            down = jnp.transpose(result).astype(jnp.bfloat16)
            for number, h in enumerate(chunk):
                stage[step, :, h * DH : (h + 1) * DH] = down[number * BLOCK : (number + 1) * BLOCK]
        add_terms(total, spots, terms * DH ** (-0.5))
        copies.append(send_tile(stage, out_ref, step, sems))
    finish(total, keep_ref, ship_ref)
    for copy in copies:
        copy.wait()


def dquery_kernel(size, dscores_ref, rows_ref, dquery_ref, stage, sems):
    copies = []
    for step in range(stage.shape[0]):
        for chunk in chunks_of(dquery_ref.shape[1] // DH, size):
            columns = slice(chunk[0] * BLOCK, (chunk[-1] + 1) * BLOCK)
            across = dot(rows_ref[step], dscores_ref[step, :, columns], 0, 0) * DH ** (-0.5)
            down = jnp.transpose(across).astype(jnp.bfloat16)
            for number, h in enumerate(chunk):
                rows = slice(number * BLOCK, (number + 1) * BLOCK)
                stage[step, :, h * DH : (h + 1) * DH] = down[rows]
        copies.append(send_tile(stage, dquery_ref, step, sems))
    for copy in copies:
        copy.wait()


def small_grant():
    return pltpu.CompilerParams(vmem_limit_bytes=8 * 1024 * 1024)


def kernel_options(products, pairs):
    return {
        "compiler_params": pltpu.CompilerParams(vmem_limit_bytes=36 * 1024 * 1024),
        "cost_estimate": pl.CostEstimate(
            flops=4 * products * pairs * DH, bytes_accessed=4 * pairs, transcendentals=pairs
        ),
    }


def whole_body(queries, keys, values, d_out, rand_blocks, glob_blocks):
    seq_count = lax.axis_size("seq")
    head_count = lax.axis_size("head")
    short = keys.shape[0]
    tok_count, width = queries.shape
    heads_here = width // DH
    blocks_here = tok_count // BLOCK
    pair_count = seq_count // 2
    listed = (3 + GLOB + RAND) * BLOCK
    columns = heads_here * BLOCK
    pairs = blocks_here * listed * columns
    size = heads_here

    smem = pl.BlockSpec(memory_space=pltpu.SMEM)
    anywhere = pl.BlockSpec(memory_space=pl.ANY)
    tile_shape = jax.ShapeDtypeStruct(queries.shape, jnp.bfloat16)
    piece = jax.ShapeDtypeStruct((2 * short, DH), jnp.bfloat16)
    spots_shape = jax.ShapeDtypeStruct((blocks_here, 3 + GLOB + RAND), jnp.int32)
    rand_blocks, glob_blocks, keys, values, queries, d_out = [
        pltpu.with_memory_space_constraint(x, pltpu.HBM)
        for x in (rand_blocks, glob_blocks, keys, values, queries, d_out)
    ]
    pieces = pl.pallas_call(
        pack_kernel,
        in_specs=[anywhere] * 2,
        out_specs=[anywhere] * head_count,
        out_shape=[piece] * head_count,
        scratch_shapes=[pltpu.SemaphoreType.DMA((2 * head_count,))],
        compiler_params=small_grant(),
    )(keys, values)
    pieces = [pieces[0]] + [
        lax.ppermute(pieces[k], "head", flips(head_count, k)) for k in range(1, head_count)
    ]

    def along_far(own):
        parts = [own]
        for k in range(2, seq_count, 2):
            parts.append(lax.ppermute(own, "seq", flips(seq_count, k)))
        return parts

    def to_near(part):
        return lax.ppermute(part, "seq", flips(seq_count, 1))

    key_far = along_far(jnp.stack([p[:short] for p in pieces]))
    order = sorted(range(pair_count), key=lambda n: (bin(n).count("1"), -n))
    key_parts = [part for n in order for part in (key_far[n], to_near(key_far[n]))]
    key_starts = [slot * blocks_here for n in order for slot in (2 * n, 2 * n + 1)]
    value_starts = [2 * n * blocks_here for n in order]
    value_own = jnp.stack([p[short:] for p in pieces])
    value_pair = jnp.concatenate([value_own, to_near(value_own)])
    value_pair, _ = lax.optimization_barrier((value_pair, key_far[1:]))
    value_far = along_far(value_pair)
    value_parts = [value_far[n] for n in order]

    lists = pltpu.VMEM((blocks_here, listed, DH), jnp.bfloat16)
    stage = pltpu.VMEM((blocks_here, BLOCK, width), jnp.bfloat16)
    tile_sems = pltpu.SemaphoreType.DMA((blocks_here,))
    vmem = pl.BlockSpec(memory_space=pltpu.VMEM)
    half = (pair_count, blocks_here, BLOCK, DH)
    square_shape = jax.ShapeDtypeStruct((blocks_here, listed, columns), jnp.bfloat16)
    listing_shape = jax.ShapeDtypeStruct((blocks_here, listed, DH), jnp.bfloat16)
    keep_shape = jax.ShapeDtypeStruct(half, jnp.float32)
    ship_shape = jax.ShapeDtypeStruct(half, jnp.bfloat16)
    library = pltpu.VMEM((seq_count * blocks_here, BLOCK, DH), jnp.bfloat16)
    total = pltpu.VMEM((seq_count * blocks_here, BLOCK, DH), jnp.float32)

    probs, key_lists, value_keep, value_ship, spots, query_here, grad_here = pl.pallas_call(
        lambda *refs: probs_kernel(seq_count, key_starts, size, *refs),
        in_specs=[anywhere] * 4 + [vmem] * len(key_parts),
        out_specs=[vmem] * 4 + [smem] + [vmem] * 2,
        out_shape=[
            square_shape,
            listing_shape,
            keep_shape,
            ship_shape,
            spots_shape,
            tile_shape,
            tile_shape,
        ],
        scratch_shapes=[
            library,
            total,
            pltpu.SMEM(rand_blocks.shape, jnp.int32),
            pltpu.SMEM(glob_blocks.shape, jnp.int32),
            pltpu.SemaphoreType.DMA((4,)),
        ],
        **kernel_options(2, pairs),
    )(rand_blocks, glob_blocks, queries, d_out, *key_parts)
    value_near = lax.ppermute(value_ship, "seq", flips(seq_count, 1))
    attn_out, dscores, key_keep, key_ship = pl.pallas_call(
        lambda *refs: dscores_kernel(value_starts, size, *refs),
        in_specs=[smem, vmem, vmem, vmem] + [vmem] * len(value_parts),
        out_specs=[anywhere, vmem, vmem, vmem],
        out_shape=[tile_shape, square_shape, keep_shape, ship_shape],
        scratch_shapes=[library, total, lists, stage, tile_sems],
        **kernel_options(3, pairs),
    )(spots, query_here, grad_here, probs, *value_parts)
    key_near = lax.ppermute(key_ship, "seq", flips(seq_count, 1))

    def sums_of(keep, near):
        sums = keep + near.astype(jnp.float32)
        return sums[0], [sums[pair].astype(jnp.bfloat16) for pair in range(1, pair_count)]

    def from_far(sums):
        return [
            lax.ppermute(sums[pair - 1], "seq", flips(seq_count, 2 * pair))
            for pair in order[1:]
        ]

    def added(own, far):
        for part in far:
            own = own + part.astype(jnp.float32)
        return own

    key_own, key_sums = sums_of(key_keep, key_near)
    key_far = from_far(key_sums)
    value_own, value_sums = sums_of(value_keep, value_near)
    value_terms = from_far(value_sums)
    d_queries = pl.pallas_call(
        lambda *refs: dquery_kernel(size, *refs),
        in_specs=[vmem, vmem],
        out_specs=anywhere,
        out_shape=tile_shape,
        scratch_shapes=[stage, tile_sems],
        **kernel_options(1, pairs),
    )(*lax.optimization_barrier((dscores, key_lists, key_sums))[:2])

    key_far, value_terms, d_queries = lax.optimization_barrier((key_far, value_terms, d_queries))
    packed = jnp.concatenate(
        [added(key_own, key_far), added(value_own, value_terms)], axis=1
    ).astype(jnp.bfloat16)
    back = [
        lax.ppermute(packed[k], "head", flips(head_count, k)) if k else packed[0]
        for k in head_order(head_count)
    ]
    flat = jax.ShapeDtypeStruct(keys.shape, jnp.bfloat16)
    d_keys, d_values = pl.pallas_call(
        unpack_kernel, out_shape=[flat, flat], compiler_params=small_grant()
    )(*back)
    return (attn_out, d_queries, d_keys, d_values)


def body(queries, keys, values, d_out, rand_blocks, glob_blocks):
    seq_count = lax.axis_size("seq")
    head_count = lax.axis_size("head")
    blocks_here = rand_blocks.shape[0]
    capacity = -(-rand_blocks.size // seq_count)
    powers = all(n & (n - 1) == 0 for n in (seq_count, head_count))
    fits = keys.shape[0] == BLOCK and blocks_here == head_count
    if capacity >= blocks_here and seq_count > 1 and powers and fits:
        return whole_body(queries, keys, values, d_out, rand_blocks, glob_blocks)
    return request_body(queries, keys, values, d_out, rand_blocks, glob_blocks)


def solution(mesh):
    in_specs = (
        P("seq", "head"),
        P(("seq", "head"), None),
        P(("seq", "head"), None),
        P("seq", "head"),
        P("seq", None),
        P(),
    )
    out_specs = (
        P("seq", "head"),
        P("seq", "head"),
        P(("seq", "head"), None),
        P(("seq", "head"), None),
    )
    return jax.shard_map(body, mesh=mesh, in_specs=in_specs, out_specs=out_specs, check_vma=False)
```
